256 devices in a mesh: ctx: 32 (over y, z), tp: 8 (over x, core).
Axes of the slice: x: 4, y: 4, z: 8, core: 2. Of those that a mesh axis runs over, the one named last changes fastest.
Arguments:
- inputs: bfloat16 [2, 8, 16384], P(None, None, 'ctx'), may hold values from -6 to 6
- norm_gain: float32 [16384], P('ctx'), may hold values from 0.1 to 1.9
- w_query: bfloat16 [16384, 16384], P('ctx', 'tp'), may hold values from -0.046875 to 0.046875
- w_key: bfloat16 [16384, 1024], P('ctx', 'tp'), may hold values from -0.046875 to 0.046875
- w_value: bfloat16 [16384, 1024], P('ctx', 'tp'), may hold values from -0.046875 to 0.046875
- w_out: bfloat16 [16384, 16384], P('tp', 'ctx'), may hold values from -0.046875 to 0.046875
- key_cache: bfloat16 [8, 32768, 1024], P(None, 'ctx', 'tp'), may hold values from -125 to 125
- value_cache: bfloat16 [8, 32768, 1024], P(None, 'ctx', 'tp'), may hold values from -6 to 6
Outputs:
- attended: bfloat16 [2, 8, 16384], P(None, None, 'ctx')
- new_keys: bfloat16 [2, 8, 1024], P(None, None, 'tp')
- new_values: bfloat16 [2, 8, 1024], P(None, None, 'tp')
The draws below stay inside these ranges and needn't reach their ends.
All inputs are finite; a program needn't handle non-finite values.
Results may differ from the reference program's by a relative error of at most 0.02.
Values may be sent and summed in bfloat16 or wider, within the bound.
A program may use at most 64 MiB of HBM per device.

```python
import jax
import jax.numpy as jnp
from jax import lax

D = 16384
QG = 16
HD = 128
STEPS = 2
ROWS = 8
KVH = 8
CTX = 32768


def draw_key_cache(key, part):
    key = jax.random.fold_in(key, 7)
    shape = (ROWS, CTX, KVH * HD)
    base_key, sign_key, pick_key = jax.random.split(key, 3)
    values = 3.0 * jax.random.truncated_normal(base_key, -4.0, 4.0, shape, jnp.float32)
    signs = jax.random.randint(sign_key, shape, 0, 2).astype(jnp.float32) * 2.0 - 1.0
    picked = jax.random.randint(pick_key, (ROWS, CTX, 1), 0, 16) == 0
    first_row = (jnp.arange(ROWS) == 0)[:, None, None]
    strong = 100.0 * signs + jnp.clip(values, -20.0, 20.0)
    values = jnp.where(jnp.logical_and(picked, first_row), strong, values)
    return values.astype(jnp.bfloat16)


def steps_of(key, dims, shards, smallest, largest):
    loudness, own = 1.0, jax.random.fold_in(key, 6)
    for axis_at, shards_of in shards:
        draws = jnp.exp(jax.random.uniform(jax.random.fold_in(own, axis_at), (shards_of,), jnp.float32, smallest / len(shards), largest / len(shards)))
        loudness = loudness * jnp.repeat(draws, dims[axis_at] // shards_of).reshape([-1 if axis == axis_at else 1 for axis in range(len(dims))])
    return loudness


def gaussian(stream_key, extent, spread, bound, shards=(), kind=jnp.bfloat16):
    drawn = spread * jax.random.normal(stream_key, extent, jnp.float32)
    if shards:
        drawn = drawn * steps_of(stream_key, extent, shards, -0.22, 0.18)
    return jnp.clip(drawn, -bound, bound).astype(kind)


def setup_inputs(seed: int = 0) -> dict:
    seeds = jax.random.split(jax.random.key(seed), 9)
    inputs = gaussian(seeds[0], (STEPS, ROWS, D), 1.0, 6.0, ((2, 32),))
    norm_gain = jnp.clip(1.0 + 0.18 * jax.random.normal(seeds[1], (D,), jnp.float32), 0.1, 1.9)
    w_query = gaussian(seeds[2], (D, KVH * QG * HD), D ** -0.5, 0.046875, ((0, 32), (1, 8)))
    w_key = gaussian(seeds[3], (D, KVH * HD), D ** -0.5, 0.046875, ((0, 32), (1, 8)))
    w_value = gaussian(seeds[4], (D, KVH * HD), D ** -0.5, 0.046875, ((0, 32), (1, 8)))
    w_out = gaussian(seeds[5], (KVH * QG * HD, D), (KVH * QG * HD) ** -0.5, 0.046875, ((0, 8), (1, 32)))
    key_cache = draw_key_cache(jax.random.fold_in(seeds[8], 71), 0)
    value_cache = gaussian(seeds[7], (ROWS, CTX, KVH * HD), 1.0, 6.0, ((1, 32), (2, 8)))
    return dict(inputs=inputs, norm_gain=norm_gain, w_query=w_query, w_key=w_key, w_value=w_value, w_out=w_out, key_cache=key_cache, value_cache=value_cache)


def attend_row(packed):
    query_row, cached_keys, cached_values, fresh_keys, fresh_values = packed
    all_keys = jnp.concatenate([cached_keys, fresh_keys], axis=0).astype(jnp.float32).reshape(-1, KVH, HD)
    all_values = jnp.concatenate([cached_values, fresh_values], axis=0).astype(jnp.float32).reshape(-1, KVH, HD)
    heads = query_row.astype(jnp.float32).reshape(KVH, QG, HD)
    score = jnp.einsum('gqd,tgd->gqt', heads, all_keys) * (1.0 / math_sqrt(HD))
    top = lax.optimization_barrier(jnp.max(score, axis=-1, keepdims=True))
    weight = jnp.exp(score - top)
    total = lax.optimization_barrier(jnp.sum(weight, axis=-1))
    weight_low = lax.optimization_barrier(weight.astype(jnp.bfloat16)).astype(jnp.float32)
    summed = jnp.einsum('gqt,tgd->gqd', weight_low, all_values)
    return (summed / total[..., None]).reshape(-1).astype(jnp.bfloat16)

def math_sqrt(number):
    return float(number) ** 0.5

def reference(inputs, norm_gain, w_query, w_key, w_value, w_out, key_cache, value_cache):
    attended = []
    fresh_keys = []
    fresh_values = []
    for position in range(STEPS):
        hidden = inputs[position].astype(jnp.float32)
        scaling = lax.rsqrt(lax.optimization_barrier(jnp.sum(hidden * hidden, axis=1, keepdims=True)) / D + 1e-05)
        normed = (hidden * norm_gain).astype(jnp.bfloat16)
        query = (scaling * jnp.dot(normed, w_query, preferred_element_type=jnp.float32)).astype(jnp.bfloat16)
        key_row = (scaling * jnp.dot(normed, w_key, preferred_element_type=jnp.float32)).astype(jnp.bfloat16)
        value_row = (scaling * jnp.dot(normed, w_value, preferred_element_type=jnp.float32)).astype(jnp.bfloat16)
        fresh_keys.append(key_row)
        fresh_values.append(value_row)
        stacked_keys = jnp.stack(fresh_keys, axis=1)
        stacked_values = jnp.stack(fresh_values, axis=1)
        heads_out = lax.map(attend_row, (query, key_cache, value_cache, stacked_keys, stacked_values))
        attended.append(jnp.dot(heads_out, w_out, preferred_element_type=jnp.float32).astype(jnp.bfloat16))
    return (jnp.stack(attended), jnp.stack(fresh_keys), jnp.stack(fresh_values))
```

```python
import functools

import jax
import jax.numpy as jnp
from jax import lax
from jax.experimental import pallas as pl
from jax.experimental.pallas import tpu as pltpu
from jax.sharding import PartitionSpec as P

QG = 16
HD = 128
STEPS = 2
ROWS = 8
M = STEPS * ROWS
TILES = QG + 2
LOG2E = 1.4426950408889634
F32 = jnp.float32
BF16 = jnp.bfloat16


def owner_of(tile):
    y, j = tile // 4, lax.rem(tile, 4)
    head_owner = y * 8 + 2 * j + lax.rem(y, 2)
    return jnp.where(tile < QG, head_owner, jnp.where(tile == QG, 1, 21))


def tile_of(me):
    y, z = me // 8, lax.rem(me, 8)
    head = y * 4 + z // 2
    other = jnp.where(me == 1, QG, jnp.where(me == 21, QG + 1, TILES))
    return jnp.where(lax.rem(y + z, 2) == 0, head, other)


def kernel(
    nctx,
    ntp,
    x_hbm,
    gain_hbm,
    wq_hbm,
    wk_hbm,
    wv_hbm,
    wo_hbm,
    kc_hbm,
    vc_hbm,
    att_ref,
    nk_ref,
    nv_ref,
    x_v,
    gain_v,
    w_v,
    wo_v,
    kc_v,
    vc_v,
    sq_src,
    sq_buf,
    part_src,
    part_buf,
    proj_src,
    proj_buf,
    q_rows,
    o_rows,
    p_v,
    st_src,
    st_buf,
    o_src,
    o_buf,
    ho_src,
    ho_buf,
    fin_buf,
    load_sem,
    send_sem,
    recv_sem,
):
    me = lax.axis_index("ctx")
    tp = lax.axis_index("tp")
    depth = x_v.shape[2]
    width = wo_v.shape[1]
    mine = tile_of(me)
    owns_head = mine < QG
    owns = mine < TILES
    SQ, PART, PROJ, PROJ_KV, ST, OUT, HO, FIN = range(8)

    def load(i, src, dst):
        copy = pltpu.make_async_copy(src, dst, load_sem.at[i])
        copy.start()
        return copy

    load_x = load(0, x_hbm, x_v)
    load_gain = load(1, gain_hbm, gain_v)
    load_q = load(2, wq_hbm, w_v.at[:, pl.ds(0, QG * HD)])
    load_k = load(3, wk_hbm, w_v.at[:, pl.ds(QG * HD, HD)])
    load_v = load(4, wv_hbm, w_v.at[:, pl.ds(QG * HD + HD, HD)])
    load_kc = load(5, kc_hbm, kc_v)
    load_vc = load(6, vc_hbm, vc_v)
    load_wo = load(7, wo_hbm, wo_v)

    barrier = pltpu.get_barrier_semaphore()
    for i in range(1, nctx):
        pl.semaphore_signal(barrier, inc=1, device_id={"ctx": lax.rem(me + i, nctx)})
    for i in range(1, ntp):
        pl.semaphore_signal(barrier, inc=1, device_id={"tp": lax.rem(tp + i, ntp)})

    def send(src, dst, phase, recv, **where):
        pltpu.make_async_remote_copy(
            src_ref=src,
            dst_ref=dst,
            send_sem=send_sem.at[phase],
            recv_sem=recv_sem.at[recv],
            device_id=where,
        ).start()

    def keep(src, dst, recv):
        pltpu.make_async_copy(src, dst, recv_sem.at[recv]).start()

    def await_bytes(ref, sem):
        pltpu.make_async_copy(ref, ref, sem).wait()

    load_x.wait()
    load_gain.wait()
    x = jnp.concatenate([x_v[0].astype(F32), x_v[1].astype(F32)], axis=0)
    normed = (x * gain_v[...]).astype(BF16)
    diagonal = lax.broadcasted_iota(jnp.int32, (M, HD), 0) == lax.broadcasted_iota(
        jnp.int32, (M, HD), 1
    )
    squares = jnp.sum(x * x, axis=1, keepdims=True)
    sq_src[...] = jnp.sum(jnp.where(diagonal, squares, 0.0), axis=0, keepdims=True)
    load_q.wait()
    load_k.wait()
    load_v.wait()
    part = jnp.dot(normed, w_v[...], preferred_element_type=F32)
    for h in range(TILES):
        part_src[h] = part[:, h * HD : (h + 1) * HD]

    pl.semaphore_wait(barrier, nctx - 1 + ntp - 1)

    @pl.when(owns)
    def _():
        keep(part_src.at[mine], part_buf.at[me], PART)
        keep(sq_src, sq_buf.at[me], SQ)

    for i in range(TILES):
        h = lax.rem(me + i, TILES)
        to = owner_of(h)

        @pl.when(to != me)
        def _():
            send(part_src.at[h], part_buf.at[me], PART, PART, ctx=to)
            send(sq_src, sq_buf.at[me], SQ, SQ, ctx=to)

    @pl.when(owns)
    def _():
        await_bytes(sq_buf, recv_sem.at[SQ])
        await_bytes(part_buf, recv_sem.at[PART])
        total = jnp.sum(sq_buf[...], axis=0)
        total = jnp.sum(jnp.where(diagonal, total, 0.0), axis=1, keepdims=True)
        scaling = lax.rsqrt(total / (depth * nctx) + 1e-05)
        proj_src[...] = (scaling * jnp.sum(part_buf[...], axis=0)).astype(BF16)
        group = jnp.where(owns_head, PROJ, PROJ_KV)
        keep(proj_src, proj_buf.at[mine], group)
        for i in range(1, nctx):
            send(proj_src, proj_buf.at[mine], PROJ, group, ctx=lax.rem(me + i, nctx))

    await_bytes(proj_buf.at[pl.ds(0, QG)], recv_sem.at[PROJ])
    for h in range(QG):
        q_rows[pl.ds(h * M, M), :] = proj_buf[h].astype(F32)
    load_kc.wait()
    score_scale = LOG2E / float(HD) ** 0.5
    lane = lax.broadcasted_iota(jnp.int32, (QG, HD), 1)
    stats = jnp.zeros((QG, HD), F32)
    inverse = []
    for r in range(ROWS):
        q = jnp.concatenate(
            [q_rows[pl.ds(s * ROWS + r, QG, stride=M), :] for s in range(STEPS)], axis=0
        ).astype(BF16)
        score = lax.dot_general(
            q, kc_v[r], (((1,), (1,)), ((), ())), preferred_element_type=F32
        )
        top = jnp.max(score, axis=1, keepdims=True)
        weight = jnp.exp2((score - top) * score_scale)
        total = jnp.sum(weight, axis=1, keepdims=True)
        p_v[r] = weight.astype(BF16)
        inverse.append(1.0 / total)
        lse = top * score_scale + jnp.log2(total)
        for s in range(STEPS):
            stats = jnp.where(lane == s * ROWS + r, lse[s * QG : (s + 1) * QG], stats)
    for h in range(QG):
        st_src[h] = stats[h : h + 1]

    @pl.when(owns_head)
    def _():
        keep(st_src.at[mine], st_buf.at[me], ST)

    for i in range(QG):
        h = lax.rem(me + i, QG)
        to = owner_of(h)

        @pl.when(to != me)
        def _():
            send(st_src.at[h], st_buf.at[me], ST, ST, ctx=to)

    load_vc.wait()
    for r in range(ROWS):
        out = jnp.dot(p_v[r], vc_v[r], preferred_element_type=F32) * inverse[r]
        for s in range(STEPS):
            o_rows[pl.ds(s * ROWS + r, QG, stride=M), :] = out[s * QG : (s + 1) * QG]
    for h in range(QG):
        o_src[h] = o_rows[pl.ds(h * M, M), :].astype(BF16)

    @pl.when(owns_head)
    def _():
        keep(o_src.at[mine], o_buf.at[me], OUT)

    for i in range(QG):
        h = lax.rem(me + i, QG)
        to = owner_of(h)

        @pl.when(to != me)
        def _():
            send(o_src.at[h], o_buf.at[me], OUT, OUT, ctx=to)

    await_bytes(proj_buf.at[pl.ds(QG, 2)], recv_sem.at[PROJ_KV])
    new_k, new_v = proj_buf[QG].astype(F32), proj_buf[QG + 1].astype(F32)
    for s in range(STEPS):
        nk_ref[s] = new_k[s * ROWS : (s + 1) * ROWS].astype(BF16)
        nv_ref[s] = new_v[s * ROWS : (s + 1) * ROWS].astype(BF16)

    @pl.when(owns_head)
    def _():
        second = lax.broadcasted_iota(jnp.int32, (M, 1), 0) >= ROWS
        q = proj_src[...].astype(F32)
        k0 = jnp.concatenate([new_k[:ROWS]] * 2, axis=0)
        k1 = jnp.concatenate([new_k[ROWS:]] * 2, axis=0)
        v0 = jnp.concatenate([new_v[:ROWS]] * 2, axis=0)
        v1 = jnp.concatenate([new_v[ROWS:]] * 2, axis=0)
        f0 = jnp.sum(q * k0, axis=1, keepdims=True) * score_scale
        f1 = jnp.sum(q * k1, axis=1, keepdims=True) * score_scale
        await_bytes(st_buf, recv_sem.at[ST])
        lse = jnp.transpose(st_buf[...].reshape(nctx, HD))[:M]
        top = jnp.maximum(jnp.max(lse, axis=1, keepdims=True), f0)
        top = jnp.maximum(top, jnp.where(second, f1, f0))
        share = jnp.exp2(lse - top)
        w0 = jnp.exp2(f0 - top)
        w1 = jnp.where(second, jnp.exp2(jnp.where(second, f1, f0) - top), 0.0)
        over = 1.0 / (jnp.sum(share, axis=1, keepdims=True) + w0 + w1)
        joined = w0 * v0 + w1 * v1
        await_bytes(o_buf, recv_sem.at[OUT])
        for c in range(nctx):
            joined += share[:, c : c + 1] * o_buf[c].astype(F32)
        ho_src[...] = (joined * over).astype(BF16)
        keep(ho_src, ho_buf.at[mine], HO)
        for i in range(1, nctx):
            send(ho_src, ho_buf.at[mine], HO, HO, ctx=lax.rem(me + i, nctx))

    load_wo.wait()
    await_bytes(ho_buf, recv_sem.at[HO])
    heads_out = jnp.concatenate([ho_buf[h] for h in range(QG)], axis=1)
    y = jnp.dot(heads_out, wo_v[...], preferred_element_type=F32)
    fin_buf[tp] = y.astype(BF16)
    for i in range(1, ntp):
        send(fin_buf.at[tp], fin_buf.at[tp], FIN, FIN, tp=lax.rem(tp + i, ntp))
    await_bytes(fin_buf.at[pl.ds(0, ntp - 1)], recv_sem.at[FIN])
    att = jnp.sum(fin_buf[...].astype(F32), axis=0)
    for s in range(STEPS):
        att_ref[s] = att[s * ROWS : (s + 1) * ROWS].astype(BF16)

    @pl.when(owns)
    def _():
        await_bytes(part_src.at[pl.ds(0, TILES - 1)], send_sem.at[PART])
        await_bytes(sq_buf.at[pl.ds(0, TILES - 1)], send_sem.at[SQ])
        await_bytes(o_buf.at[pl.ds(0, nctx - 1)], send_sem.at[PROJ])

    @pl.when(jnp.logical_not(owns))
    def _():
        await_bytes(part_src, send_sem.at[PART])
        await_bytes(sq_buf.at[pl.ds(0, TILES)], send_sem.at[SQ])

    @pl.when(owns_head)
    def _():
        await_bytes(st_src.at[pl.ds(0, QG - 1)], send_sem.at[ST])
        await_bytes(o_src.at[pl.ds(0, QG - 1)], send_sem.at[OUT])
        await_bytes(o_buf.at[pl.ds(0, nctx - 1)], send_sem.at[HO])

    @pl.when(jnp.logical_not(owns_head))
    def _():
        await_bytes(st_src, send_sem.at[ST])
        await_bytes(o_src, send_sem.at[OUT])

    await_bytes(fin_buf.at[pl.ds(0, ntp - 1)], send_sem.at[FIN])


def local(nctx, ntp, inputs, norm_gain, w_query, w_key, w_value, w_out, key_cache, value_cache):
    depth = inputs.shape[2]
    width = w_out.shape[1]
    cached = key_cache.shape[1]
    hbm = pl.BlockSpec(memory_space=pl.ANY)
    vmem = pl.BlockSpec(memory_space=pltpu.VMEM)
    return pl.pallas_call(
        functools.partial(kernel, nctx, ntp),
        out_shape=(
            jax.ShapeDtypeStruct((STEPS, ROWS, width), BF16),
            jax.ShapeDtypeStruct((STEPS, ROWS, HD), BF16),
            jax.ShapeDtypeStruct((STEPS, ROWS, HD), BF16),
        ),
        in_specs=[hbm] * 8,
        out_specs=(vmem,) * 3,
        scratch_shapes=[
            pltpu.VMEM((STEPS, ROWS, depth), BF16),
            pltpu.VMEM((1, depth), F32),
            pltpu.VMEM((depth, TILES * HD), BF16),
            pltpu.VMEM((QG * HD, width), BF16),
            pltpu.VMEM((ROWS, cached, HD), BF16),
            pltpu.VMEM((ROWS, cached, HD), BF16),
            pltpu.VMEM((1, HD), F32),
            pltpu.VMEM((nctx, 1, HD), F32),
            pltpu.VMEM((TILES, M, HD), F32),
            pltpu.VMEM((nctx, M, HD), F32),
            pltpu.VMEM((M, HD), BF16),
            pltpu.VMEM((TILES, M, HD), BF16),
            pltpu.VMEM((QG * M, HD), F32),
            pltpu.VMEM((QG * M, HD), F32),
            pltpu.VMEM((ROWS, STEPS * QG, cached), BF16),
            pltpu.VMEM((QG, 1, HD), F32),
            pltpu.VMEM((nctx, 1, HD), F32),
            pltpu.VMEM((QG, M, HD), BF16),
            pltpu.VMEM((nctx, M, HD), BF16),
            pltpu.VMEM((M, HD), BF16),
            pltpu.VMEM((QG, M, HD), BF16),
            pltpu.VMEM((ntp, M, width), BF16),
            pltpu.SemaphoreType.DMA((8,)),
            pltpu.SemaphoreType.DMA((8,)),
            pltpu.SemaphoreType.DMA((8,)),
        ],
        compiler_params=pltpu.CompilerParams(
            collective_id=0, has_side_effects=True, vmem_limit_bytes=48 * 1024 * 1024
        ),
    )(
        inputs,
        norm_gain.reshape(1, depth),
        w_query,
        w_key,
        w_value,
        w_out,
        key_cache,
        value_cache,
    )


def solution(mesh):
    placed = (
        P(None, None, "ctx"),
        P("ctx"),
        P("ctx", "tp"),
        P("ctx", "tp"),
        P("ctx", "tp"),
        P("tp", "ctx"),
        P(None, "ctx", "tp"),
        P(None, "ctx", "tp"),
    )
    return jax.shard_map(
        functools.partial(local, mesh.shape["ctx"], mesh.shape["tp"]),
        mesh=mesh,
        in_specs=placed,
        out_specs=(P(None, None, "ctx"), P(None, None, "tp"), P(None, None, "tp")),
        check_vma=False,
    )
```

```python
import functools

import jax
import jax.numpy as jnp
from jax import lax
from jax.experimental import pallas as pl
from jax.experimental.pallas import tpu as pltpu
from jax.sharding import PartitionSpec as P

QG = 16
HD = 128
STEPS = 2
ROWS = 8
M = STEPS * ROWS
TILES = QG + 2
LOG2E = 1.4426950408889634
F32 = jnp.float32
BF16 = jnp.bfloat16


STEPS_AWAY = sorted(
    ((dy, dz) for dy in range(4) for dz in range(8) if (dy, dz) != (0, 0)),
    key=lambda step: -(min(step[0], 4 - step[0]) + min(step[1], 8 - step[1])),
)
NEAR = 4
KEY_OWNER, VALUE_OWNER = 0, 8


def kernel(
    nctx,
    ntp,
    x_hbm,
    gain_hbm,
    wq_hbm,
    wk_hbm,
    wv_hbm,
    wo_hbm,
    kc_hbm,
    vc_hbm,
    att_ref,
    nk_ref,
    nv_ref,
    x_v,
    gain_v,
    wq_v,
    wkv_v,
    wo_v,
    kc_v,
    vc_v,
    sq_src,
    sq_buf,
    part_src,
    part_buf,
    kv_buf,
    proj_src,
    kv_src,
    proj_buf,
    q_rows,
    o_rows,
    p_v,
    st_src,
    st_buf,
    o_src,
    o_buf,
    ho_src,
    ho_buf,
    fin_buf,
    load_sem,
    send_sem,
    recv_sem,
):
    me = lax.axis_index("ctx")
    tp = lax.axis_index("tp")
    y, z = me // 8, lax.rem(me, 8)
    depth = x_v.shape[2]
    mine = y * NEAR + z
    owns = z < NEAR
    SQ, PART, PART_KV, PROJ, PROJ_KV, ST, OUT, HO, FIN = range(9)

    def load(i, src, dst):
        copy = pltpu.make_async_copy(src, dst, load_sem.at[i])
        copy.start()
        return copy

    load_x = load(0, x_hbm, x_v)
    load_gain = load(1, gain_hbm, gain_v)
    chunk = depth // 4
    load_q = [
        load(2 + i, wq_hbm.at[pl.ds(i * chunk, chunk)], wq_v.at[pl.ds(i * chunk, chunk)])
        for i in range(4)
    ]
    load_k = load(6, wk_hbm, wkv_v.at[:, pl.ds(0, HD)])
    load_v = load(7, wv_hbm, wkv_v.at[:, pl.ds(HD, HD)])

    def others():
        for dy, dz in STEPS_AWAY:
            ty, tz = lax.rem(y + dy, 4), lax.rem(z + dz, 8)
            yield ty * 8 + tz, ty * NEAR + tz, tz < NEAR

    tp_others = [
        lax.rem(tp + i, ntp) for i in sorted(range(1, ntp), key=lambda i: abs(i - ntp / 2))
    ]

    barrier = pltpu.get_barrier_semaphore()

    @pl.when(owns)
    def _():
        for to, _, _ in others():
            pl.semaphore_signal(barrier, inc=1, device_id={"ctx": to})

    for to in tp_others:
        pl.semaphore_signal(barrier, inc=1, device_id={"tp": to})

    def send(src, dst, phase, recv, **where):
        pltpu.make_async_remote_copy(
            src_ref=src,
            dst_ref=dst,
            send_sem=send_sem.at[phase],
            recv_sem=recv_sem.at[recv],
            device_id=where,
        ).start()

    def keep(src, dst, recv):
        pltpu.make_async_copy(src, dst, recv_sem.at[recv]).start()

    def await_bytes(ref, sem):
        pltpu.make_async_copy(ref, ref, sem).wait()

    load_x.wait()
    load_gain.wait()
    x = jnp.concatenate([x_v[0].astype(F32), x_v[1].astype(F32)], axis=0)
    normed = (x * gain_v[...]).astype(BF16)
    diagonal = lax.broadcasted_iota(jnp.int32, (M, HD), 0) == lax.broadcasted_iota(
        jnp.int32, (M, HD), 1
    )
    squares = jnp.sum(x * x, axis=1, keepdims=True)
    sq_src[...] = jnp.sum(jnp.where(diagonal, squares, 0.0), axis=0, keepdims=True)
    for copy in load_q:
        copy.wait()
    load_k.wait()
    load_v.wait()
    load_kc = load(0, kc_hbm, kc_v)
    load_vc = load(1, vc_hbm, vc_v)
    load_wo = load(2, wo_hbm, wo_v)
    part = jnp.dot(normed, wq_v[...], preferred_element_type=F32)
    for h in range(QG):
        part_src[h] = part[:, h * HD : (h + 1) * HD]
    part = jnp.dot(normed, wkv_v[...], preferred_element_type=F32)
    for h in range(2):
        part_src[QG + h] = part[:, h * HD : (h + 1) * HD]

    @pl.when(owns)
    def _():
        pl.semaphore_wait(barrier, QG - 1 + ntp - 1)

    @pl.when(jnp.logical_not(owns))
    def _():
        pl.semaphore_wait(barrier, QG + ntp - 1)

    for to, h, is_owner in others():

        @pl.when(is_owner)
        def _():
            send(part_src.at[h], part_buf.at[me], PART, PART, ctx=to)
            send(sq_src, sq_buf.at[me], SQ, SQ, ctx=to)

    @pl.when(owns)
    def _():
        keep(part_src.at[mine], part_buf.at[me], PART)
        keep(sq_src, sq_buf.at[me], SQ)

    for tile, owner in ((QG, KEY_OWNER), (QG + 1, VALUE_OWNER)):

        @pl.when(me != owner)
        def _():
            send(part_src.at[tile], kv_buf.at[me], PART_KV, PART_KV, ctx=owner)

        @pl.when(me == owner)
        def _():
            keep(part_src.at[tile], kv_buf.at[me], PART_KV)

    @pl.when(owns)
    def _():
        await_bytes(sq_buf, recv_sem.at[SQ])
        total = jnp.sum(sq_buf[...], axis=0)
        total = jnp.sum(jnp.where(diagonal, total, 0.0), axis=1, keepdims=True)
        scaling = lax.rsqrt(total / (depth * nctx) + 1e-05)
        await_bytes(part_buf, recv_sem.at[PART])
        proj_src[...] = (scaling * jnp.sum(part_buf[...], axis=0)).astype(BF16)
        for to, _, _ in others():
            send(proj_src, proj_buf.at[mine], PROJ, PROJ, ctx=to)
        keep(proj_src, proj_buf.at[mine], PROJ)

        for tile, owner in ((QG, KEY_OWNER), (QG + 1, VALUE_OWNER)):

            @pl.when(me == owner)
            def _():
                await_bytes(kv_buf, recv_sem.at[PART_KV])
                kv_src[...] = (scaling * jnp.sum(kv_buf[...], axis=0)).astype(BF16)
                for to, _, _ in others():
                    send(kv_src, proj_buf.at[tile], PROJ_KV, PROJ_KV, ctx=to)
                keep(kv_src, proj_buf.at[tile], PROJ_KV)

    await_bytes(proj_buf.at[pl.ds(0, QG)], recv_sem.at[PROJ])
    for h in range(QG):
        q_rows[pl.ds(h * M, M), :] = proj_buf[h].astype(F32)
    load_kc.wait()
    score_scale = LOG2E / float(HD) ** 0.5
    lane = lax.broadcasted_iota(jnp.int32, (QG, HD), 1)
    stats = jnp.zeros((QG, HD), F32)
    inverse = []
    for r in range(ROWS):
        q = jnp.concatenate(
            [q_rows[pl.ds(s * ROWS + r, QG, stride=M), :] for s in range(STEPS)], axis=0
        ).astype(BF16)
        score = lax.dot_general(
            q, kc_v[r], (((1,), (1,)), ((), ())), preferred_element_type=F32
        )
        top = jnp.max(score, axis=1, keepdims=True)
        weight = jnp.exp2((score - top) * score_scale)
        total = jnp.sum(weight, axis=1, keepdims=True)
        p_v[r] = weight.astype(BF16)
        inverse.append(1.0 / total)
        lse = top * score_scale + jnp.log2(total)
        for s in range(STEPS):
            stats = jnp.where(lane == s * ROWS + r, lse[s * QG : (s + 1) * QG], stats)
    for h in range(QG):
        st_src[h] = stats[h : h + 1]

    for to, h, is_owner in others():

        @pl.when(is_owner)
        def _():
            send(st_src.at[h], st_buf.at[me], ST, ST, ctx=to)

    @pl.when(owns)
    def _():
        keep(st_src.at[mine], st_buf.at[me], ST)

    load_vc.wait()
    for r in range(ROWS):
        out = jnp.dot(p_v[r], vc_v[r], preferred_element_type=F32) * inverse[r]
        for s in range(STEPS):
            o_rows[pl.ds(s * ROWS + r, QG, stride=M), :] = out[s * QG : (s + 1) * QG]
    for h in range(QG):
        o_src[h] = o_rows[pl.ds(h * M, M), :].astype(BF16)

    for to, h, is_owner in others():

        @pl.when(is_owner)
        def _():
            send(o_src.at[h], o_buf.at[me], OUT, OUT, ctx=to)

    @pl.when(owns)
    def _():
        keep(o_src.at[mine], o_buf.at[me], OUT)

    await_bytes(proj_buf.at[pl.ds(QG, 2)], recv_sem.at[PROJ_KV])
    new_k, new_v = proj_buf[QG].astype(F32), proj_buf[QG + 1].astype(F32)
    for s in range(STEPS):
        nk_ref[s] = new_k[s * ROWS : (s + 1) * ROWS].astype(BF16)
        nv_ref[s] = new_v[s * ROWS : (s + 1) * ROWS].astype(BF16)

    @pl.when(owns)
    def _():
        second = lax.broadcasted_iota(jnp.int32, (M, 1), 0) >= ROWS
        q = proj_src[...].astype(F32)
        k0 = jnp.concatenate([new_k[:ROWS]] * 2, axis=0)
        k1 = jnp.concatenate([new_k[ROWS:]] * 2, axis=0)
        v0 = jnp.concatenate([new_v[:ROWS]] * 2, axis=0)
        v1 = jnp.concatenate([new_v[ROWS:]] * 2, axis=0)
        f0 = jnp.sum(q * k0, axis=1, keepdims=True) * score_scale
        f1 = jnp.sum(q * k1, axis=1, keepdims=True) * score_scale
        await_bytes(st_buf, recv_sem.at[ST])
        lse = jnp.transpose(st_buf[...].reshape(nctx, HD))[:M]
        top = jnp.maximum(jnp.max(lse, axis=1, keepdims=True), f0)
        top = jnp.maximum(top, jnp.where(second, f1, f0))
        share = jnp.exp2(lse - top)
        w0 = jnp.exp2(f0 - top)
        w1 = jnp.where(second, jnp.exp2(jnp.where(second, f1, f0) - top), 0.0)
        over = 1.0 / (jnp.sum(share, axis=1, keepdims=True) + w0 + w1)
        joined = w0 * v0 + w1 * v1
        await_bytes(o_buf, recv_sem.at[OUT])
        for c in range(nctx):
            joined += share[:, c : c + 1] * o_buf[c].astype(F32)
        ho_src[...] = (joined * over).astype(BF16)
        for to, _, _ in others():
            send(ho_src, ho_buf.at[mine], HO, HO, ctx=to)
        keep(ho_src, ho_buf.at[mine], HO)

    load_wo.wait()
    await_bytes(ho_buf, recv_sem.at[HO])
    heads_out = jnp.concatenate([ho_buf[h] for h in range(QG)], axis=1)
    y = jnp.dot(heads_out, wo_v[...], preferred_element_type=F32)
    fin_buf[tp] = y.astype(BF16)
    for to in tp_others:
        send(fin_buf.at[tp], fin_buf.at[tp], FIN, FIN, tp=to)
    await_bytes(fin_buf.at[pl.ds(0, ntp - 1)], recv_sem.at[FIN])
    att = jnp.sum(fin_buf[...].astype(F32), axis=0)
    for s in range(STEPS):
        att_ref[s] = att[s * ROWS : (s + 1) * ROWS].astype(BF16)

    @pl.when(owns)
    def _():
        await_bytes(part_src.at[pl.ds(0, QG - 1)], send_sem.at[PART])
        await_bytes(sq_buf.at[pl.ds(0, QG - 1)], send_sem.at[SQ])
        await_bytes(o_buf.at[pl.ds(0, nctx - 1)], send_sem.at[PROJ])
        await_bytes(st_src.at[pl.ds(0, QG - 1)], send_sem.at[ST])
        await_bytes(o_src.at[pl.ds(0, QG - 1)], send_sem.at[OUT])
        await_bytes(o_buf.at[pl.ds(0, nctx - 1)], send_sem.at[HO])

    @pl.when(jnp.logical_not(owns))
    def _():
        await_bytes(part_src.at[pl.ds(0, QG)], send_sem.at[PART])
        await_bytes(sq_buf.at[pl.ds(0, QG)], send_sem.at[SQ])
        await_bytes(st_src, send_sem.at[ST])
        await_bytes(o_src, send_sem.at[OUT])

    owns_kv = jnp.logical_or(me == KEY_OWNER, me == VALUE_OWNER)

    @pl.when(owns_kv)
    def _():
        await_bytes(part_src.at[pl.ds(0, 1)], send_sem.at[PART_KV])
        await_bytes(o_buf.at[pl.ds(0, nctx - 1)], send_sem.at[PROJ_KV])

    @pl.when(jnp.logical_not(owns_kv))
    def _():
        await_bytes(part_src.at[pl.ds(0, 2)], send_sem.at[PART_KV])

    await_bytes(fin_buf.at[pl.ds(0, ntp - 1)], send_sem.at[FIN])


def local(nctx, ntp, inputs, norm_gain, w_query, w_key, w_value, w_out, key_cache, value_cache):
    depth = inputs.shape[2]
    width = w_out.shape[1]
    cached = key_cache.shape[1]
    hbm = pl.BlockSpec(memory_space=pltpu.HBM)
    vmem = pl.BlockSpec(memory_space=pltpu.VMEM)
    shapes = (
        jax.ShapeDtypeStruct((STEPS, ROWS, width), BF16),
        jax.ShapeDtypeStruct((STEPS, ROWS, HD), BF16),
        jax.ShapeDtypeStruct((STEPS, ROWS, HD), BF16),
    )
    results = pl.pallas_call(
        functools.partial(kernel, nctx, ntp),
        out_shape=shapes,
        in_specs=[hbm] * 8,
        out_specs=(vmem,) * 3,
        scratch_shapes=[
            pltpu.VMEM((STEPS, ROWS, depth), BF16),
            pltpu.VMEM((1, depth), F32),
            pltpu.VMEM((depth, QG * HD), BF16),
            pltpu.VMEM((depth, 2 * HD), BF16),
            pltpu.VMEM((QG * HD, width), BF16),
            pltpu.VMEM((ROWS, cached, HD), BF16),
            pltpu.VMEM((ROWS, cached, HD), BF16),
            pltpu.VMEM((1, HD), F32),
            pltpu.VMEM((nctx, 1, HD), F32),
            pltpu.VMEM((TILES, M, HD), F32),
            pltpu.VMEM((nctx, M, HD), F32),
            pltpu.VMEM((nctx, M, HD), F32),
            pltpu.VMEM((M, HD), BF16),
            pltpu.VMEM((M, HD), BF16),
            pltpu.VMEM((TILES, M, HD), BF16),
            pltpu.VMEM((QG * M, HD), F32),
            pltpu.VMEM((QG * M, HD), F32),
            pltpu.VMEM((ROWS, STEPS * QG, cached), BF16),
            pltpu.VMEM((QG, 1, HD), F32),
            pltpu.VMEM((nctx, 1, HD), F32),
            pltpu.VMEM((QG, M, HD), BF16),
            pltpu.VMEM((nctx, M, HD), BF16),
            pltpu.VMEM((M, HD), BF16),
            pltpu.VMEM((QG, M, HD), BF16),
            pltpu.VMEM((ntp, M, width), BF16),
            pltpu.SemaphoreType.DMA((8,)),
            pltpu.SemaphoreType.DMA((9,)),
            pltpu.SemaphoreType.DMA((9,)),
        ],
        compiler_params=pltpu.CompilerParams(
            collective_id=0, has_side_effects=True, vmem_limit_bytes=40 * 1024 * 1024
        ),
    )(
        *(
            pltpu.with_memory_space_constraint(operand, pltpu.HBM)
            for operand in (
                inputs,
                norm_gain.reshape(1, depth),
                w_query,
                w_key,
                w_value,
                w_out,
                key_cache,
                value_cache,
            )
        )
    )
    return results


def solution(mesh):
    placed = (
        P(None, None, "ctx"),
        P("ctx"),
        P("ctx", "tp"),
        P("ctx", "tp"),
        P("ctx", "tp"),
        P("tp", "ctx"),
        P(None, "ctx", "tp"),
        P(None, "ctx", "tp"),
    )
    return jax.shard_map(
        functools.partial(local, mesh.shape["ctx"], mesh.shape["tp"]),
        mesh=mesh,
        in_specs=placed,
        out_specs=(P(None, None, "ctx"), P(None, None, "tp"), P(None, None, "tp")),
        check_vma=False,
    )
```

```python
import functools

import jax
import jax.numpy as jnp
from jax import lax
from jax.experimental import pallas as pl
from jax.experimental.pallas import tpu as pltpu
from jax.sharding import PartitionSpec as P

QG = 16
HD = 128
STEPS = 2
ROWS = 8
M = STEPS * ROWS
TILES = QG + 2
LOG2E = 1.4426950408889634
F32 = jnp.float32
BF16 = jnp.bfloat16


STEPS_AWAY = sorted(
    ((dy, dz) for dy in range(4) for dz in range(8) if (dy, dz) != (0, 0)),
    key=lambda step: -(min(step[0], 4 - step[0]) + min(step[1], 8 - step[1])),
)
def kernel(
    nctx,
    ntp,
    x_hbm,
    gain_hbm,
    wq_hbm,
    wk_hbm,
    wv_hbm,
    wo_hbm,
    kc_hbm,
    vc_hbm,
    out_ref,
    x_v,
    gain_v,
    wq_v,
    wkv_v,
    wo_v,
    kc_v,
    vc_v,
    sq_src,
    sq_buf,
    part_src,
    part_buf,
    kv_buf,
    proj_src,
    kv_src,
    proj_buf,
    q_rows,
    o_rows,
    p_v,
    st_src,
    st_buf,
    o_src,
    o_buf,
    ho_src,
    ho_buf,
    fin_buf,
    load_sem,
    send_sem,
    recv_sem,
):
    me = lax.axis_index("ctx")
    tp = lax.axis_index("tp")
    y, z, core = me // 8, lax.rem(me, 8), lax.rem(tp, 2)
    chip_tp = tp - core
    depth = x_v.shape[2]
    width = wo_v.shape[1]
    SQ, PART, PART_KV, PROJ, PROJ_KV, ST, OUT, HO, FIN = range(9)

    parity = lax.rem(y + z, 2)
    tile = y * 4 + z // 2
    sums = core == 1
    sums_kv = jnp.logical_and(sums, jnp.logical_and(y < 2, z < 2))
    own_sum = jnp.logical_and(sums, parity == 1)
    sibling_sum = jnp.logical_and(core == 0, parity == 0)
    group_tp = chip_tp + parity
    near = lax.rem(z + 1, 8)
    head = y * 4 + near
    joins = near < 4

    def others():
        for dy, dz in STEPS_AWAY:
            ty, tz = lax.rem(y + dy, 4), lax.rem(z + dz, 8)
            yield ty * 8 + tz, ty, tz

    tp_others = [
        lax.rem(tp + i, ntp) for i in sorted(range(1, ntp), key=lambda i: abs(i - ntp / 2))
    ]

    barrier = pltpu.get_barrier_semaphore()

    @pl.when(sums)
    def _():
        for to, _, _ in others():
            pl.semaphore_signal(barrier, inc=1, device_id={"ctx": to, "tp": group_tp})

        @pl.when(parity == 0)
        def _():
            pl.semaphore_signal(barrier, inc=1, device_id={"ctx": me, "tp": group_tp})

    for to in tp_others:
        pl.semaphore_signal(barrier, inc=1, device_id={"tp": to})

    def load(i, src, dst):
        copy = pltpu.make_async_copy(src, dst, load_sem.at[i])
        copy.start()
        return copy

    load_x = load(0, x_hbm, x_v)
    load_gain = load(1, gain_hbm, gain_v)
    chunk = depth // 4
    load_q = [
        load(2 + i, wq_hbm.at[pl.ds(i * chunk, chunk)], wq_v.at[pl.ds(i * chunk, chunk)])
        for i in range(4)
    ]
    load_k = load(6, wk_hbm, wkv_v.at[:, pl.ds(0, HD)])
    load_v = load(7, wv_hbm, wkv_v.at[:, pl.ds(HD, HD)])

    def send(src, dst, phase, recv, **where):
        pltpu.make_async_remote_copy(
            src_ref=src,
            dst_ref=dst,
            send_sem=send_sem.at[phase],
            recv_sem=recv_sem.at[recv],
            device_id=where,
        ).start()

    def keep(src, dst, recv):
        pltpu.make_async_copy(src, dst, recv_sem.at[recv]).start()

    def await_bytes(ref, sem):
        pltpu.make_async_copy(ref, ref, sem).wait()

    load_x.wait()
    load_gain.wait()
    x = jnp.concatenate([x_v[0].astype(F32), x_v[1].astype(F32)], axis=0)
    normed = (x * gain_v[...]).astype(BF16)
    diagonal = lax.broadcasted_iota(jnp.int32, (M, HD), 0) == lax.broadcasted_iota(
        jnp.int32, (M, HD), 1
    )
    squares = jnp.sum(x * x, axis=1, keepdims=True)
    sq_src[...] = jnp.sum(jnp.where(diagonal, squares, 0.0), axis=0, keepdims=True)
    for copy in load_q:
        copy.wait()
    load_k.wait()
    load_v.wait()
    load_kc = load(0, kc_hbm, kc_v)
    load_vc = load(1, vc_hbm, vc_v)
    load_wo = load(2, wo_hbm, wo_v)
    part = jnp.dot(normed, wq_v[...], preferred_element_type=F32)
    for h in range(QG):
        part_src[h] = part[:, h * HD : (h + 1) * HD]
    part = jnp.dot(normed, wkv_v[...], preferred_element_type=F32)
    for h in range(2):
        part_src[QG + h] = part[:, h * HD : (h + 1) * HD]

    @pl.when(own_sum)
    def _():
        pl.semaphore_wait(barrier, QG - 1 + ntp - 1)

    @pl.when(jnp.logical_not(own_sum))
    def _():
        pl.semaphore_wait(barrier, QG + ntp - 1)

    for to, ty, tz in others():

        @pl.when(lax.rem(ty + tz, 2) == core)
        def _():
            h = ty * 4 + tz // 2
            send(part_src.at[h], part_buf.at[me], PART, PART, ctx=to, tp=chip_tp + 1)
            send(sq_src, sq_buf.at[me], SQ, SQ, ctx=to, tp=chip_tp + 1)

    @pl.when(sibling_sum)
    def _():
        send(part_src.at[tile], part_buf.at[me], PART, PART, tp=chip_tp + 1)
        send(sq_src, sq_buf.at[me], SQ, SQ, tp=chip_tp + 1)

    @pl.when(own_sum)
    def _():
        keep(part_src.at[tile], part_buf.at[me], PART)
        keep(sq_src, sq_buf.at[me], SQ)

    own_kv = jnp.logical_and(sums_kv, own_sum)
    for i in range(2):
        to = 8 * i + lax.rem(i + core, 2)
        stays = jnp.logical_and(own_kv, y == i)

        @pl.when(stays)
        def _():
            keep(part_src.at[QG + i], kv_buf.at[me], PART_KV)

        @pl.when(jnp.logical_not(stays))
        def _():
            send(part_src.at[QG + i], kv_buf.at[me], PART_KV, PART_KV, ctx=to, tp=chip_tp + 1)

    def broadcast(src, dst, phase):
        for to, _, _ in others():
            send(src, dst, phase, phase, ctx=to, tp=group_tp)

        @pl.when(parity == 0)
        def _():
            send(src, dst, phase, phase, tp=group_tp)

        @pl.when(parity == 1)
        def _():
            keep(src, dst, phase)

    @pl.when(sums)
    def _():
        await_bytes(sq_buf, recv_sem.at[SQ])
        total = jnp.sum(sq_buf[...], axis=0)
        total = jnp.sum(jnp.where(diagonal, total, 0.0), axis=1, keepdims=True)
        scaling = lax.rsqrt(total / (depth * nctx) + 1e-05)
        await_bytes(part_buf, recv_sem.at[PART])
        proj_src[...] = (scaling * jnp.sum(part_buf[...], axis=0)).astype(BF16)
        broadcast(proj_src, proj_buf.at[tile], PROJ)

        @pl.when(sums_kv)
        def _():
            await_bytes(kv_buf, recv_sem.at[PART_KV])
            kv_src[...] = (scaling * jnp.sum(kv_buf[...], axis=0)).astype(BF16)
            broadcast(kv_src, proj_buf.at[QG + y], PROJ_KV)

    await_bytes(proj_buf.at[pl.ds(0, QG)], recv_sem.at[PROJ])
    for h in range(QG):
        q_rows[pl.ds(h * M, M), :] = proj_buf[h].astype(F32)
    load_kc.wait()
    score_scale = LOG2E / float(HD) ** 0.5
    lane = lax.broadcasted_iota(jnp.int32, (QG, HD), 1)
    stats = jnp.zeros((QG, HD), F32)
    inverse = []
    for r in range(ROWS):
        q = jnp.concatenate(
            [q_rows[pl.ds(s * ROWS + r, QG, stride=M), :] for s in range(STEPS)], axis=0
        ).astype(BF16)
        score = lax.dot_general(
            q, kc_v[r], (((1,), (1,)), ((), ())), preferred_element_type=F32
        )
        top = jnp.max(score, axis=1, keepdims=True)
        weight = jnp.exp2((score - top) * score_scale)
        total = jnp.sum(weight, axis=1, keepdims=True)
        p_v[r] = weight.astype(BF16)
        inverse.append(1.0 / total)
        lse = top * score_scale + jnp.log2(total)
        for s in range(STEPS):
            stats = jnp.where(lane == s * ROWS + r, lse[s * QG : (s + 1) * QG], stats)
    for h in range(QG):
        st_src[h] = stats[h : h + 1]

    for to, ty, tz in others():
        to_near = lax.rem(tz + 1, 8)

        @pl.when(to_near < 4)
        def _():
            send(st_src.at[ty * 4 + to_near], st_buf.at[me], ST, ST, ctx=to)

    @pl.when(joins)
    def _():
        keep(st_src.at[head], st_buf.at[me], ST)

    load_vc.wait()
    for r in range(ROWS):
        out = jnp.dot(p_v[r], vc_v[r], preferred_element_type=F32) * inverse[r]
        for s in range(STEPS):
            o_rows[pl.ds(s * ROWS + r, QG, stride=M), :] = out[s * QG : (s + 1) * QG]
    for h in range(QG):
        o_src[h] = o_rows[pl.ds(h * M, M), :].astype(BF16)

    for to, ty, tz in others():
        to_near = lax.rem(tz + 1, 8)

        @pl.when(to_near < 4)
        def _():
            send(o_src.at[ty * 4 + to_near], o_buf.at[me], OUT, OUT, ctx=to)

    @pl.when(joins)
    def _():
        keep(o_src.at[head], o_buf.at[me], OUT)

    await_bytes(proj_buf.at[pl.ds(QG, 2)], recv_sem.at[PROJ_KV])
    new_k, new_v = proj_buf[QG].astype(F32), proj_buf[QG + 1].astype(F32)
    for s in range(STEPS):
        out_ref[s, :, width : width + HD] = new_k[s * ROWS : (s + 1) * ROWS].astype(BF16)
        out_ref[s, :, width + HD :] = new_v[s * ROWS : (s + 1) * ROWS].astype(BF16)

    @pl.when(joins)
    def _():
        second = lax.broadcasted_iota(jnp.int32, (M, 1), 0) >= ROWS
        q = proj_buf[head].astype(F32)
        k0 = jnp.concatenate([new_k[:ROWS]] * 2, axis=0)
        k1 = jnp.concatenate([new_k[ROWS:]] * 2, axis=0)
        v0 = jnp.concatenate([new_v[:ROWS]] * 2, axis=0)
        v1 = jnp.concatenate([new_v[ROWS:]] * 2, axis=0)
        f0 = jnp.sum(q * k0, axis=1, keepdims=True) * score_scale
        f1 = jnp.sum(q * k1, axis=1, keepdims=True) * score_scale
        await_bytes(st_buf, recv_sem.at[ST])
        lse = jnp.transpose(st_buf[...].reshape(nctx, HD))[:M]
        top = jnp.maximum(jnp.max(lse, axis=1, keepdims=True), f0)
        top = jnp.maximum(top, jnp.where(second, f1, f0))
        share = jnp.exp2(lse - top)
        w0 = jnp.exp2(f0 - top)
        w1 = jnp.where(second, jnp.exp2(jnp.where(second, f1, f0) - top), 0.0)
        over = 1.0 / (jnp.sum(share, axis=1, keepdims=True) + w0 + w1)
        joined = w0 * v0 + w1 * v1
        await_bytes(o_buf, recv_sem.at[OUT])
        for c in range(nctx):
            joined += share[:, c : c + 1] * o_buf[c].astype(F32)
        ho_src[...] = (joined * over).astype(BF16)
        for to, _, _ in others():
            send(ho_src, ho_buf.at[head], HO, HO, ctx=to)
        keep(ho_src, ho_buf.at[head], HO)

    load_wo.wait()
    await_bytes(ho_buf, recv_sem.at[HO])
    heads_out = jnp.concatenate([ho_buf[h] for h in range(QG)], axis=1)
    y = jnp.dot(heads_out, wo_v[...], preferred_element_type=F32)
    fin_buf[tp] = y.astype(BF16)
    for to in tp_others:
        send(fin_buf.at[tp], fin_buf.at[tp], FIN, FIN, tp=to)
    await_bytes(fin_buf.at[pl.ds(0, ntp - 1)], recv_sem.at[FIN])
    att = jnp.sum(fin_buf[...].astype(F32), axis=0)
    for s in range(STEPS):
        out_ref[s, :, :width] = att[s * ROWS : (s + 1) * ROWS].astype(BF16)

    @pl.when(own_sum)
    def _():
        await_bytes(part_src.at[pl.ds(0, QG - 1)], send_sem.at[PART])
        await_bytes(sq_buf.at[pl.ds(0, QG - 1)], send_sem.at[SQ])

    @pl.when(jnp.logical_not(own_sum))
    def _():
        await_bytes(part_src.at[pl.ds(0, QG)], send_sem.at[PART])
        await_bytes(sq_buf.at[pl.ds(0, QG)], send_sem.at[SQ])

    @pl.when(own_kv)
    def _():
        await_bytes(part_src.at[pl.ds(0, 1)], send_sem.at[PART_KV])

    @pl.when(jnp.logical_not(own_kv))
    def _():
        await_bytes(part_src.at[pl.ds(0, 2)], send_sem.at[PART_KV])

    for does, phase in ((sums, PROJ), (sums_kv, PROJ_KV)):

        @pl.when(jnp.logical_and(does, parity == 1))
        def _():
            await_bytes(o_buf.at[pl.ds(0, nctx - 1)], send_sem.at[phase])

        @pl.when(jnp.logical_and(does, parity == 0))
        def _():
            await_bytes(o_buf, send_sem.at[phase])

    @pl.when(joins)
    def _():
        await_bytes(st_src.at[pl.ds(0, QG - 1)], send_sem.at[ST])
        await_bytes(o_src.at[pl.ds(0, QG - 1)], send_sem.at[OUT])
        await_bytes(o_buf.at[pl.ds(0, nctx - 1)], send_sem.at[HO])

    @pl.when(jnp.logical_not(joins))
    def _():
        await_bytes(st_src, send_sem.at[ST])
        await_bytes(o_src, send_sem.at[OUT])

    await_bytes(fin_buf.at[pl.ds(0, ntp - 1)], send_sem.at[FIN])


def local(nctx, ntp, inputs, norm_gain, w_query, w_key, w_value, w_out, key_cache, value_cache):
    depth = inputs.shape[2]
    width = w_out.shape[1]
    cached = key_cache.shape[1]
    hbm = pl.BlockSpec(memory_space=pltpu.HBM)
    vmem = pl.BlockSpec(memory_space=pltpu.VMEM)
    results = pl.pallas_call(
        functools.partial(kernel, nctx, ntp),
        out_shape=jax.ShapeDtypeStruct((STEPS, ROWS, width + 2 * HD), BF16),
        in_specs=[hbm] * 8,
        out_specs=vmem,
        scratch_shapes=[
            pltpu.VMEM((STEPS, ROWS, depth), BF16),
            pltpu.VMEM((1, depth), F32),
            pltpu.VMEM((depth, QG * HD), BF16),
            pltpu.VMEM((depth, 2 * HD), BF16),
            pltpu.VMEM((QG * HD, width), BF16),
            pltpu.VMEM((ROWS, cached, HD), BF16),
            pltpu.VMEM((ROWS, cached, HD), BF16),
            pltpu.VMEM((1, HD), F32),
            pltpu.VMEM((nctx, 1, HD), F32),
            pltpu.VMEM((TILES, M, HD), F32),
            pltpu.VMEM((nctx, M, HD), F32),
            pltpu.VMEM((nctx, M, HD), F32),
            pltpu.VMEM((M, HD), BF16),
            pltpu.VMEM((M, HD), BF16),
            pltpu.VMEM((TILES, M, HD), BF16),
            pltpu.VMEM((QG * M, HD), F32),
            pltpu.VMEM((QG * M, HD), F32),
            pltpu.VMEM((ROWS, STEPS * QG, cached), BF16),
            pltpu.VMEM((QG, 1, HD), F32),
            pltpu.VMEM((nctx, 1, HD), F32),
            pltpu.VMEM((QG, M, HD), BF16),
            pltpu.VMEM((nctx, M, HD), BF16),
            pltpu.VMEM((M, HD), BF16),
            pltpu.VMEM((QG, M, HD), BF16),
            pltpu.VMEM((ntp, M, width), BF16),
            pltpu.SemaphoreType.DMA((8,)),
            pltpu.SemaphoreType.DMA((9,)),
            pltpu.SemaphoreType.DMA((9,)),
        ],
        compiler_params=pltpu.CompilerParams(
            collective_id=0, has_side_effects=True, vmem_limit_bytes=40 * 1024 * 1024
        ),
    )(
        *(
            pltpu.with_memory_space_constraint(operand, pltpu.HBM)
            for operand in (
                inputs,
                norm_gain.reshape(1, depth),
                w_query,
                w_key,
                w_value,
                w_out,
                key_cache,
                value_cache,
            )
        )
    )
    return (
        results[:, :, :width],
        results[:, :, width : width + HD],
        results[:, :, width + HD :],
    )


def solution(mesh):
    placed = (
        P(None, None, "ctx"),
        P("ctx"),
        P("ctx", "tp"),
        P("ctx", "tp"),
        P("ctx", "tp"),
        P("tp", "ctx"),
        P(None, "ctx", "tp"),
        P(None, "ctx", "tp"),
    )
    return jax.shard_map(
        functools.partial(local, mesh.shape["ctx"], mesh.shape["tp"]),
        mesh=mesh,
        in_specs=placed,
        out_specs=(P(None, None, "ctx"), P(None, None, "tp"), P(None, None, "tp")),
        check_vma=False,
    )
```

```python
import functools

import jax
import jax.numpy as jnp
from jax import lax
from jax.experimental import pallas as pl
from jax.experimental.pallas import tpu as pltpu
from jax.sharding import PartitionSpec as P

QG = 16
HD = 128
STEPS = 2
ROWS = 8
M = STEPS * ROWS
TILES = QG + 2
LOG2E = 1.4426950408889634
F32 = jnp.float32
BF16 = jnp.bfloat16


STEPS_AWAY = sorted(
    ((dy, dz) for dy in range(4) for dz in range(8) if (dy, dz) != (0, 0)),
    key=lambda step: -(min(step[0], 4 - step[0]) + min(step[1], 8 - step[1])),
)
def head_of(y, z):
    near = lax.rem(z + 2, 8)
    low = jnp.where(near < 6, y * 6 + near, QG)
    return jnp.where(y < 2, low, jnp.where(y == 3, jnp.where(z < 3, 12 + z, QG), 15 + z))


def kernel(
    nctx,
    ntp,
    x_hbm,
    gain_hbm,
    wq_hbm,
    wk_hbm,
    wv_hbm,
    wo_hbm,
    kc_hbm,
    vc_hbm,
    out_ref,
    x_v,
    gain_v,
    wq_v,
    wkv_v,
    wo_v,
    kc_v,
    kt_v,
    vc_v,
    sq_src,
    sq_buf,
    part_src,
    part_buf,
    kv_buf,
    proj_src,
    kv_src,
    proj_buf,
    q_rows,
    o_rows,
    p_v,
    st_src,
    st_buf,
    o_src,
    o_buf,
    ho_src,
    ho_buf,
    fin_buf,
    load_sem,
    send_sem,
    recv_sem,
):
    me = lax.axis_index("ctx")
    tp = lax.axis_index("tp")
    y, z, core = me // 8, lax.rem(me, 8), lax.rem(tp, 2)
    chip_tp = tp - core
    depth = x_v.shape[2]
    width = wo_v.shape[1]
    SQ, PART, PART_KV, PROJ, PROJ_KV, ST, OUT, HO, FIN = range(9)

    parity = lax.rem(y + z, 2)
    tile = y * 4 + z // 2
    sums = core == 1
    sums_kv = jnp.logical_and(sums, jnp.logical_and(y < 2, z < 2))
    own_sum = jnp.logical_and(sums, parity == 1)
    sibling_sum = jnp.logical_and(core == 0, parity == 0)
    group_tp = chip_tp + parity
    head = head_of(y, z)
    joins = head < QG

    def others():
        for dy, dz in STEPS_AWAY:
            ty, tz = lax.rem(y + dy, 4), lax.rem(z + dz, 8)
            yield ty * 8 + tz, ty, tz

    x = tp // 2
    tp_steps = [(i, k) for k in (1, 0) for i in (2, 1, 3, 0)]

    barrier = pltpu.get_barrier_semaphore()

    @pl.when(sums)
    def _():
        for to, _, _ in others():
            pl.semaphore_signal(barrier, inc=1, device_id={"ctx": to, "tp": group_tp})

        @pl.when(parity == 0)
        def _():
            pl.semaphore_signal(barrier, inc=1, device_id={"ctx": me, "tp": group_tp})

    for i in range(1, ntp):
        pl.semaphore_signal(barrier, inc=1, device_id={"tp": lax.rem(tp + i, ntp)})

    def load(i, src, dst):
        copy = pltpu.make_async_copy(src, dst, load_sem.at[i])
        copy.start()
        return copy

    load_x = load(0, x_hbm, x_v)
    load_gain = load(1, gain_hbm, gain_v)
    chunk = depth // 4
    load_q = [
        load(2 + i, wq_hbm.at[pl.ds(i * chunk, chunk)], wq_v.at[pl.ds(i * chunk, chunk)])
        for i in range(4)
    ]
    load_k = load(6, wk_hbm, wkv_v.at[:, pl.ds(0, HD)])
    load_v = load(7, wv_hbm, wkv_v.at[:, pl.ds(HD, HD)])

    def send(src, dst, phase, recv, **where):
        pltpu.make_async_remote_copy(
            src_ref=src,
            dst_ref=dst,
            send_sem=send_sem.at[phase],
            recv_sem=recv_sem.at[recv],
            device_id=where,
        ).start()

    def keep(src, dst, recv):
        pltpu.make_async_copy(src, dst, recv_sem.at[recv]).start()

    def await_bytes(ref, sem):
        pltpu.make_async_copy(ref, ref, sem).wait()

    load_x.wait()
    load_gain.wait()
    hidden = jnp.concatenate([x_v[0].astype(F32), x_v[1].astype(F32)], axis=0)
    normed = (hidden * gain_v[...]).astype(BF16)
    diagonal = lax.broadcasted_iota(jnp.int32, (M, HD), 0) == lax.broadcasted_iota(
        jnp.int32, (M, HD), 1
    )
    squares = jnp.sum(hidden * hidden, axis=1, keepdims=True)
    sq_src[...] = jnp.sum(jnp.where(diagonal, squares, 0.0), axis=0, keepdims=True)
    for copy in load_q:
        copy.wait()
    load_k.wait()
    load_v.wait()
    load_kc = load(0, kc_hbm, kc_v)
    load_vc = load(1, vc_hbm, vc_v)
    load_wo = load(2, wo_hbm, wo_v)
    part = jnp.dot(normed, wq_v[...], preferred_element_type=F32)
    for h in range(QG):
        part_src[h] = part[:, h * HD : (h + 1) * HD]
    part = jnp.dot(normed, wkv_v[...], preferred_element_type=F32)
    for h in range(2):
        part_src[QG + h] = part[:, h * HD : (h + 1) * HD]

    @pl.when(own_sum)
    def _():
        pl.semaphore_wait(barrier, QG - 1 + ntp - 1)

    @pl.when(jnp.logical_not(own_sum))
    def _():
        pl.semaphore_wait(barrier, QG + ntp - 1)

    for odd in range(2):

        @pl.when(lax.rem(core + parity, 2) == odd)
        def _():
            for dy, dz in STEPS_AWAY:
                if (dy + dz) % 2 == odd:
                    ty, tz = lax.rem(y + dy, 4), lax.rem(z + dz, 8)
                    to, h = ty * 8 + tz, ty * 4 + tz // 2
                    send(part_src.at[h], part_buf.at[me], PART, PART, ctx=to, tp=chip_tp + 1)
                    send(sq_src, sq_buf.at[me], SQ, SQ, ctx=to, tp=chip_tp + 1)

    @pl.when(sibling_sum)
    def _():
        send(part_src.at[tile], part_buf.at[me], PART, PART, tp=chip_tp + 1)
        send(sq_src, sq_buf.at[me], SQ, SQ, tp=chip_tp + 1)

    @pl.when(own_sum)
    def _():
        keep(part_src.at[tile], part_buf.at[me], PART)
        keep(sq_src, sq_buf.at[me], SQ)

    load_kc.wait()

    @pl.loop(0, ROWS)
    def _(r):
        kt_v[r] = jnp.transpose(kc_v[r])

    def scale_of_rows():
        total = jnp.sum(sq_buf[...], axis=0)
        total = jnp.sum(jnp.where(diagonal, total, 0.0), axis=1, keepdims=True)
        return lax.rsqrt(total / (depth * nctx) + 1e-05)

    def broadcast(src, dst, phase):
        for to, _, _ in others():
            send(src, dst, phase, phase, ctx=to, tp=group_tp)

        @pl.when(parity == 0)
        def _():
            send(src, dst, phase, phase, tp=group_tp)

        @pl.when(parity == 1)
        def _():
            keep(src, dst, phase)

    @pl.when(sums)
    def _():
        await_bytes(sq_buf, recv_sem.at[SQ])
        scaling = scale_of_rows()
        await_bytes(part_buf, recv_sem.at[PART])
        proj_src[...] = (scaling * jnp.sum(part_buf[...], axis=0)).astype(BF16)
        broadcast(proj_src, proj_buf.at[tile], PROJ)

    own_kv = jnp.logical_and(sums_kv, own_sum)
    for i in range(2):
        to = 8 * i + lax.rem(i + core, 2)
        stays = jnp.logical_and(own_kv, y == i)

        @pl.when(stays)
        def _():
            keep(part_src.at[QG + i], kv_buf.at[me], PART_KV)

        @pl.when(jnp.logical_not(stays))
        def _():
            send(part_src.at[QG + i], kv_buf.at[me], PART_KV, PART_KV, ctx=to, tp=chip_tp + 1)

    await_bytes(proj_buf.at[pl.ds(0, QG)], recv_sem.at[PROJ])
    for h in range(QG):
        q_rows[pl.ds(h * M, M), :] = proj_buf[h].astype(F32)
    score_scale = LOG2E / float(HD) ** 0.5
    lane = lax.broadcasted_iota(jnp.int32, (QG, HD), 1)
    stats = jnp.zeros((QG, HD), F32)
    inverse = []
    for r in range(ROWS):
        q = jnp.concatenate(
            [q_rows[pl.ds(s * ROWS + r, QG, stride=M), :] for s in range(STEPS)], axis=0
        ).astype(BF16)
        score = jnp.dot(q, kt_v[r], preferred_element_type=F32)
        top = jnp.max(score, axis=1, keepdims=True)
        weight = jnp.exp2((score - top) * score_scale)
        total = jnp.sum(weight, axis=1, keepdims=True)
        p_v[r] = weight.astype(BF16)
        inverse.append(1.0 / total)
        lse = top * score_scale + jnp.log2(total)
        for s in range(STEPS):
            stats = jnp.where(lane == s * ROWS + r, lse[s * QG : (s + 1) * QG], stats)
    for h in range(QG):
        st_src[h] = stats[h : h + 1]

    for to, ty, tz in others():
        h = head_of(ty, tz)

        @pl.when(h < QG)
        def _():
            send(st_src.at[h], st_buf.at[me], ST, ST, ctx=to)

    @pl.when(joins)
    def _():
        keep(st_src.at[head], st_buf.at[me], ST)

    load_vc.wait()
    for r in range(ROWS):
        out = jnp.dot(p_v[r], vc_v[r], preferred_element_type=F32) * inverse[r]
        for s in range(STEPS):
            o_rows[pl.ds(s * ROWS + r, QG, stride=M), :] = out[s * QG : (s + 1) * QG]
    for h in range(QG):
        o_src[h] = o_rows[pl.ds(h * M, M), :].astype(BF16)

    for to, ty, tz in others():
        h = head_of(ty, tz)

        @pl.when(h < QG)
        def _():
            send(o_src.at[h], o_buf.at[me], OUT, OUT, ctx=to)

    @pl.when(joins)
    def _():
        keep(o_src.at[head], o_buf.at[me], OUT)

    @pl.when(sums_kv)
    def _():
        await_bytes(kv_buf, recv_sem.at[PART_KV])
        kv_src[...] = (scale_of_rows() * jnp.sum(kv_buf[...], axis=0)).astype(BF16)
        broadcast(kv_src, proj_buf.at[QG + y], PROJ_KV)

    await_bytes(proj_buf.at[pl.ds(QG, 2)], recv_sem.at[PROJ_KV])
    new_k, new_v = proj_buf[QG].astype(F32), proj_buf[QG + 1].astype(F32)
    for s in range(STEPS):
        out_ref[s, :, width : width + HD] = new_k[s * ROWS : (s + 1) * ROWS].astype(BF16)
        out_ref[s, :, width + HD :] = new_v[s * ROWS : (s + 1) * ROWS].astype(BF16)

    @pl.when(joins)
    def _():
        second = lax.broadcasted_iota(jnp.int32, (M, 1), 0) >= ROWS
        q = proj_buf[head].astype(F32)
        k0 = jnp.concatenate([new_k[:ROWS]] * 2, axis=0)
        k1 = jnp.concatenate([new_k[ROWS:]] * 2, axis=0)
        v0 = jnp.concatenate([new_v[:ROWS]] * 2, axis=0)
        v1 = jnp.concatenate([new_v[ROWS:]] * 2, axis=0)
        f0 = jnp.sum(q * k0, axis=1, keepdims=True) * score_scale
        f1 = jnp.sum(q * k1, axis=1, keepdims=True) * score_scale
        await_bytes(st_buf, recv_sem.at[ST])
        lse = jnp.transpose(st_buf[...].reshape(nctx, HD))[:M]
        top = jnp.maximum(jnp.max(lse, axis=1, keepdims=True), f0)
        top = jnp.maximum(top, jnp.where(second, f1, f0))
        share = jnp.exp2(lse - top)
        w0 = jnp.exp2(f0 - top)
        w1 = jnp.where(second, jnp.exp2(jnp.where(second, f1, f0) - top), 0.0)
        over = 1.0 / (jnp.sum(share, axis=1, keepdims=True) + w0 + w1)
        joined = w0 * v0 + w1 * v1
        await_bytes(o_buf, recv_sem.at[OUT])
        for c in range(nctx):
            joined += share[:, c : c + 1] * o_buf[c].astype(F32)
        ho_src[...] = (joined * over).astype(BF16)
        @pl.when(me != 0)
        def _():
            send(ho_src, ho_buf.at[head], HO, HO, ctx=0)

        for to, _, _ in others():

            @pl.when(to != 0)
            def _():
                send(ho_src, ho_buf.at[head], HO, HO, ctx=to)

        keep(ho_src, ho_buf.at[head], HO)

    load_wo.wait()
    await_bytes(ho_buf, recv_sem.at[HO])
    heads_out = jnp.concatenate([ho_buf[h] for h in range(QG)], axis=1)
    y = jnp.dot(heads_out, wo_v[...], preferred_element_type=F32)
    fin_buf[tp] = y.astype(BF16)
    for i, k in tp_steps:
        to = 2 * lax.rem(x + i, 4) + k
        if i == 0:

            @pl.when(to != tp)
            def _():
                send(fin_buf.at[tp], fin_buf.at[tp], FIN, FIN, tp=to)

        else:
            send(fin_buf.at[tp], fin_buf.at[tp], FIN, FIN, tp=to)
    await_bytes(fin_buf.at[pl.ds(0, ntp - 1)], recv_sem.at[FIN])
    att = jnp.sum(fin_buf[...].astype(F32), axis=0)
    for s in range(STEPS):
        out_ref[s, :, :width] = att[s * ROWS : (s + 1) * ROWS].astype(BF16)

    @pl.when(own_sum)
    def _():
        await_bytes(part_src.at[pl.ds(0, QG - 1)], send_sem.at[PART])
        await_bytes(sq_buf.at[pl.ds(0, QG - 1)], send_sem.at[SQ])

    @pl.when(jnp.logical_not(own_sum))
    def _():
        await_bytes(part_src.at[pl.ds(0, QG)], send_sem.at[PART])
        await_bytes(sq_buf.at[pl.ds(0, QG)], send_sem.at[SQ])

    @pl.when(own_kv)
    def _():
        await_bytes(part_src.at[pl.ds(0, 1)], send_sem.at[PART_KV])

    @pl.when(jnp.logical_not(own_kv))
    def _():
        await_bytes(part_src.at[pl.ds(0, 2)], send_sem.at[PART_KV])

    for does, phase in ((sums, PROJ), (sums_kv, PROJ_KV)):

        @pl.when(jnp.logical_and(does, parity == 1))
        def _():
            await_bytes(o_buf.at[pl.ds(0, nctx - 1)], send_sem.at[phase])

        @pl.when(jnp.logical_and(does, parity == 0))
        def _():
            await_bytes(o_buf, send_sem.at[phase])

    @pl.when(joins)
    def _():
        await_bytes(st_src.at[pl.ds(0, QG - 1)], send_sem.at[ST])
        await_bytes(o_src.at[pl.ds(0, QG - 1)], send_sem.at[OUT])
        await_bytes(o_buf.at[pl.ds(0, nctx - 1)], send_sem.at[HO])

    @pl.when(jnp.logical_not(joins))
    def _():
        await_bytes(st_src, send_sem.at[ST])
        await_bytes(o_src, send_sem.at[OUT])

    await_bytes(fin_buf.at[pl.ds(0, ntp - 1)], send_sem.at[FIN])


def local(nctx, ntp, inputs, norm_gain, w_query, w_key, w_value, w_out, key_cache, value_cache):
    depth = inputs.shape[2]
    width = w_out.shape[1]
    cached = key_cache.shape[1]
    hbm = pl.BlockSpec(memory_space=pltpu.HBM)
    vmem = pl.BlockSpec(memory_space=pltpu.VMEM)
    results = pl.pallas_call(
        functools.partial(kernel, nctx, ntp),
        out_shape=jax.ShapeDtypeStruct((STEPS, ROWS, width + 2 * HD), BF16),
        in_specs=[hbm] * 8,
        out_specs=vmem,
        scratch_shapes=[
            pltpu.VMEM((STEPS, ROWS, depth), BF16),
            pltpu.VMEM((1, depth), F32),
            pltpu.VMEM((depth, QG * HD), BF16),
            pltpu.VMEM((depth, 2 * HD), BF16),
            pltpu.VMEM((QG * HD, width), BF16),
            pltpu.VMEM((ROWS, cached, HD), BF16),
            pltpu.VMEM((ROWS, HD, cached), BF16),
            pltpu.VMEM((ROWS, cached, HD), BF16),
            pltpu.VMEM((1, HD), F32),
            pltpu.VMEM((nctx, 1, HD), F32),
            pltpu.VMEM((TILES, M, HD), F32),
            pltpu.VMEM((nctx, M, HD), F32),
            pltpu.VMEM((nctx, M, HD), F32),
            pltpu.VMEM((M, HD), BF16),
            pltpu.VMEM((M, HD), BF16),
            pltpu.VMEM((TILES, M, HD), BF16),
            pltpu.VMEM((QG * M, HD), F32),
            pltpu.VMEM((QG * M, HD), F32),
            pltpu.VMEM((ROWS, STEPS * QG, cached), BF16),
            pltpu.VMEM((QG, 1, HD), F32),
            pltpu.VMEM((nctx, 1, HD), F32),
            pltpu.VMEM((QG, M, HD), BF16),
            pltpu.VMEM((nctx, M, HD), BF16),
            pltpu.VMEM((M, HD), BF16),
            pltpu.VMEM((QG, M, HD), BF16),
            pltpu.VMEM((ntp, M, width), BF16),
            pltpu.SemaphoreType.DMA((8,)),
            pltpu.SemaphoreType.DMA((9,)),
            pltpu.SemaphoreType.DMA((9,)),
        ],
        compiler_params=pltpu.CompilerParams(
            collective_id=0, has_side_effects=True, vmem_limit_bytes=40 * 1024 * 1024
        ),
    )(
        *(
            pltpu.with_memory_space_constraint(operand, pltpu.HBM)
            for operand in (
                inputs,
                norm_gain.reshape(1, depth),
                w_query,
                w_key,
                w_value,
                w_out,
                key_cache,
                value_cache,
            )
        )
    )
    return (
        results[:, :, :width],
        results[:, :, width : width + HD],
        results[:, :, width + HD :],
    )


def solution(mesh):
    placed = (
        P(None, None, "ctx"),
        P("ctx"),
        P("ctx", "tp"),
        P("ctx", "tp"),
        P("ctx", "tp"),
        P("tp", "ctx"),
        P(None, "ctx", "tp"),
        P(None, "ctx", "tp"),
    )
    return jax.shard_map(
        functools.partial(local, mesh.shape["ctx"], mesh.shape["tp"]),
        mesh=mesh,
        in_specs=placed,
        out_specs=(P(None, None, "ctx"), P(None, None, "tp"), P(None, None, "tp")),
        check_vma=False,
    )
```

```python
import functools

import jax
import jax.numpy as jnp
from jax import lax
from jax.experimental import pallas as pl
from jax.experimental.pallas import tpu as pltpu
from jax.sharding import PartitionSpec as P

QG = 16
HD = 128
STEPS = 2
ROWS = 8
M = STEPS * ROWS
TILES = QG + 2
LOG2E = 1.4426950408889634
F32 = jnp.float32
BF16 = jnp.bfloat16


STEPS_AWAY = sorted(
    ((dy, dz) for dy in range(4) for dz in range(8) if (dy, dz) != (0, 0)),
    key=lambda step: -(min(step[0], 4 - step[0]) + min(step[1], 8 - step[1])),
)
def head_of(y, z):
    near = lax.rem(z + 2, 8)
    low = jnp.where(near < 6, y * 6 + near, QG)
    return jnp.where(y < 2, low, jnp.where(y == 3, jnp.where(z < 3, 12 + z, QG), 15 + z))


def kernel(
    nctx,
    ntp,
    x_hbm,
    gain_hbm,
    wq_hbm,
    wk_hbm,
    wv_hbm,
    wo_hbm,
    kc_hbm,
    vc_hbm,
    out_ref,
    x_v,
    gain_v,
    wq_v,
    wkv_v,
    wo_v,
    kc_v,
    kt_v,
    vc_v,
    sq_src,
    sq_buf,
    part_src,
    part_buf,
    kv_buf,
    proj_src,
    kv_src,
    proj_buf,
    q_rows,
    o_rows,
    p_v,
    st_src,
    st_buf,
    o_src,
    o_buf,
    ho_src,
    ho_buf,
    fin_buf,
    load_sem,
    send_sem,
    recv_sem,
):
    me = lax.axis_index("ctx")
    tp = lax.axis_index("tp")
    y, z, core = me // 8, lax.rem(me, 8), lax.rem(tp, 2)
    chip_tp = tp - core
    depth = x_v.shape[2]
    width = wo_v.shape[1]
    SQ, PART, PART_KV, PROJ, PROJ_KV, ST, OUT, HO, FIN = range(9)

    parity = lax.rem(y + z, 2)
    tile = y * 4 + z // 2
    sums = core == 1
    sums_kv = jnp.logical_and(sums, jnp.logical_and(y < 2, z < 2))
    own_sum = jnp.logical_and(sums, parity == 1)
    sibling_sum = jnp.logical_and(core == 0, parity == 0)
    group_tp = chip_tp + parity
    head = head_of(y, z)
    joins = head < QG

    def others():
        for dy, dz in STEPS_AWAY:
            ty, tz = lax.rem(y + dy, 4), lax.rem(z + dz, 8)
            yield ty * 8 + tz, ty, tz

    x = tp // 2
    tp_steps = [(i, k) for k in (1, 0) for i in (2, 1, 3, 0)]

    barrier = pltpu.get_barrier_semaphore()

    @pl.when(sums)
    def _():
        for to, _, _ in others():
            pl.semaphore_signal(barrier, inc=1, device_id={"ctx": to, "tp": group_tp})

        @pl.when(parity == 0)
        def _():
            pl.semaphore_signal(barrier, inc=1, device_id={"ctx": me, "tp": group_tp})

    for i in range(1, ntp):
        pl.semaphore_signal(barrier, inc=1, device_id={"tp": lax.rem(tp + i, ntp)})

    def load(i, src, dst):
        copy = pltpu.make_async_copy(src, dst, load_sem.at[i])
        copy.start()
        return copy

    load_x = load(0, x_hbm, x_v)
    load_gain = load(1, gain_hbm, gain_v)
    chunk = depth // 4
    load_q = [
        load(2 + i, wq_hbm.at[pl.ds(i * chunk, chunk)], wq_v.at[pl.ds(i * chunk, chunk)])
        for i in range(4)
    ]
    load_k = load(6, wk_hbm, wkv_v.at[:, pl.ds(0, HD)])
    load_v = load(7, wv_hbm, wkv_v.at[:, pl.ds(HD, HD)])

    def send(src, dst, phase, recv, **where):
        pltpu.make_async_remote_copy(
            src_ref=src,
            dst_ref=dst,
            send_sem=send_sem.at[phase],
            recv_sem=recv_sem.at[recv],
            device_id=where,
        ).start()

    def keep(src, dst, recv):
        pltpu.make_async_copy(src, dst, recv_sem.at[recv]).start()

    def await_bytes(ref, sem):
        pltpu.make_async_copy(ref, ref, sem).wait()

    load_x.wait()
    load_gain.wait()
    hidden = jnp.concatenate([x_v[0].astype(F32), x_v[1].astype(F32)], axis=0)
    normed = (hidden * gain_v[...]).astype(BF16)
    diagonal = lax.broadcasted_iota(jnp.int32, (M, HD), 0) == lax.broadcasted_iota(
        jnp.int32, (M, HD), 1
    )
    squares = jnp.sum(hidden * hidden, axis=1, keepdims=True)
    sq_src[...] = jnp.sum(jnp.where(diagonal, squares, 0.0), axis=0, keepdims=True)
    for copy in load_q:
        copy.wait()
    load_k.wait()
    load_v.wait()
    load_kc = load(0, kc_hbm, kc_v)
    load_vc = load(1, vc_hbm, vc_v)
    load_wo = load(2, wo_hbm, wo_v)
    part = jnp.dot(normed, wq_v[...], preferred_element_type=F32)
    for h in range(QG):
        part_src[h] = part[:, h * HD : (h + 1) * HD]
    part = jnp.dot(normed, wkv_v[...], preferred_element_type=F32)
    for h in range(2):
        part_src[QG + h] = part[:, h * HD : (h + 1) * HD]

    @pl.when(own_sum)
    def _():
        pl.semaphore_wait(barrier, QG - 1 + ntp - 1)

    @pl.when(jnp.logical_not(own_sum))
    def _():
        pl.semaphore_wait(barrier, QG + ntp - 1)

    for odd in range(2):

        @pl.when(lax.rem(core + parity, 2) == odd)
        def _():
            for dy, dz in STEPS_AWAY:
                if (dy + dz) % 2 == odd:
                    ty, tz = lax.rem(y + dy, 4), lax.rem(z + dz, 8)
                    to, h = ty * 8 + tz, ty * 4 + tz // 2
                    send(part_src.at[h], part_buf.at[me], PART, PART, ctx=to, tp=chip_tp + 1)
                    send(sq_src, sq_buf.at[me], SQ, SQ, ctx=to, tp=chip_tp + 1)

    @pl.when(sibling_sum)
    def _():
        send(part_src.at[tile], part_buf.at[me], PART, PART, tp=chip_tp + 1)
        send(sq_src, sq_buf.at[me], SQ, SQ, tp=chip_tp + 1)

    @pl.when(own_sum)
    def _():
        keep(part_src.at[tile], part_buf.at[me], PART)
        keep(sq_src, sq_buf.at[me], SQ)

    load_kc.wait()

    @pl.loop(0, ROWS)
    def _(r):
        kt_v[r] = jnp.transpose(kc_v[r])

    def scale_of_rows():
        total = jnp.sum(sq_buf[...], axis=0)
        total = jnp.sum(jnp.where(diagonal, total, 0.0), axis=1, keepdims=True)
        return lax.rsqrt(total / (depth * nctx) + 1e-05)

    def broadcast(src, dst, phase):
        for to, _, _ in others():
            send(src, dst, phase, phase, ctx=to, tp=group_tp)

        @pl.when(parity == 0)
        def _():
            send(src, dst, phase, phase, tp=group_tp)

        @pl.when(parity == 1)
        def _():
            keep(src, dst, phase)

    @pl.when(sums)
    def _():
        await_bytes(sq_buf, recv_sem.at[SQ])
        scaling = scale_of_rows()
        await_bytes(part_buf, recv_sem.at[PART])
        proj_src[...] = (scaling * jnp.sum(part_buf[...], axis=0)).astype(BF16)
        broadcast(proj_src, proj_buf.at[tile], PROJ)

    own_kv = jnp.logical_and(sums_kv, own_sum)
    for i in range(2):
        to = 8 * i + lax.rem(i + core, 2)
        stays = jnp.logical_and(own_kv, y == i)

        @pl.when(stays)
        def _():
            keep(part_src.at[QG + i], kv_buf.at[me], PART_KV)

        @pl.when(jnp.logical_not(stays))
        def _():
            send(part_src.at[QG + i], kv_buf.at[me], PART_KV, PART_KV, ctx=to, tp=chip_tp + 1)

    await_bytes(proj_buf.at[pl.ds(0, QG)], recv_sem.at[PROJ])
    for h in range(QG):
        q_rows[pl.ds(h * M, M), :] = proj_buf[h].astype(F32)
    score_scale = LOG2E / float(HD) ** 0.5
    lane = lax.broadcasted_iota(jnp.int32, (QG, HD), 1)
    stats = jnp.zeros((QG, HD), F32)
    inverse = []
    for r in range(ROWS):
        q = jnp.concatenate(
            [q_rows[pl.ds(s * ROWS + r, QG, stride=M), :] for s in range(STEPS)], axis=0
        ).astype(BF16)
        score = jnp.dot(q, kt_v[r], preferred_element_type=F32)
        top = jnp.max(score, axis=1, keepdims=True)
        weight = jnp.exp2((score - top) * score_scale)
        total = jnp.sum(weight, axis=1, keepdims=True)
        p_v[r] = weight.astype(BF16)
        inverse.append(1.0 / total)
        lse = top * score_scale + jnp.log2(total)
        for s in range(STEPS):
            stats = jnp.where(lane == s * ROWS + r, lse[s * QG : (s + 1) * QG], stats)
    for h in range(QG):
        st_src[h] = stats[h : h + 1]

    load_vc.wait()
    for r in range(ROWS):
        out = jnp.dot(p_v[r], vc_v[r], preferred_element_type=F32) * inverse[r]
        for s in range(STEPS):
            o_rows[pl.ds(s * ROWS + r, QG, stride=M), :] = out[s * QG : (s + 1) * QG]
    for h in range(QG):
        o_src[h] = o_rows[pl.ds(h * M, M), :].astype(BF16)

    for to, ty, tz in others():
        h = head_of(ty, tz)

        @pl.when(h < QG)
        def _():
            send(st_src.at[h], st_buf.at[me], ST, ST, ctx=to)
            send(o_src.at[h], o_buf.at[me], OUT, OUT, ctx=to)

    @pl.when(joins)
    def _():
        keep(st_src.at[head], st_buf.at[me], ST)
        keep(o_src.at[head], o_buf.at[me], OUT)

    @pl.when(sums_kv)
    def _():
        await_bytes(kv_buf, recv_sem.at[PART_KV])
        kv_src[...] = (scale_of_rows() * jnp.sum(kv_buf[...], axis=0)).astype(BF16)
        broadcast(kv_src, proj_buf.at[QG + y], PROJ_KV)

    await_bytes(proj_buf.at[pl.ds(QG, 2)], recv_sem.at[PROJ_KV])
    new_k, new_v = proj_buf[QG].astype(F32), proj_buf[QG + 1].astype(F32)
    for s in range(STEPS):
        out_ref[s, :, width : width + HD] = new_k[s * ROWS : (s + 1) * ROWS].astype(BF16)
        out_ref[s, :, width + HD :] = new_v[s * ROWS : (s + 1) * ROWS].astype(BF16)

    @pl.when(joins)
    def _():
        second = lax.broadcasted_iota(jnp.int32, (M, 1), 0) >= ROWS
        q = proj_buf[head].astype(F32)
        k0 = jnp.concatenate([new_k[:ROWS]] * 2, axis=0)
        k1 = jnp.concatenate([new_k[ROWS:]] * 2, axis=0)
        v0 = jnp.concatenate([new_v[:ROWS]] * 2, axis=0)
        v1 = jnp.concatenate([new_v[ROWS:]] * 2, axis=0)
        f0 = jnp.sum(q * k0, axis=1, keepdims=True) * score_scale
        f1 = jnp.sum(q * k1, axis=1, keepdims=True) * score_scale
        await_bytes(st_buf, recv_sem.at[ST])
        lse = jnp.transpose(st_buf[...].reshape(nctx, HD))[:M]
        top = jnp.maximum(jnp.max(lse, axis=1, keepdims=True), f0)
        top = jnp.maximum(top, jnp.where(second, f1, f0))
        share = jnp.exp2(lse - top)
        w0 = jnp.exp2(f0 - top)
        w1 = jnp.where(second, jnp.exp2(jnp.where(second, f1, f0) - top), 0.0)
        over = 1.0 / (jnp.sum(share, axis=1, keepdims=True) + w0 + w1)
        joined = w0 * v0 + w1 * v1
        await_bytes(o_buf, recv_sem.at[OUT])
        for c in range(nctx):
            joined += share[:, c : c + 1] * o_buf[c].astype(F32)
        ho_src[...] = (joined * over).astype(BF16)
        @pl.when(me != 0)
        def _():
            send(ho_src, ho_buf.at[head], HO, HO, ctx=0)

        for to, _, _ in others():

            @pl.when(to != 0)
            def _():
                send(ho_src, ho_buf.at[head], HO, HO, ctx=to)

        keep(ho_src, ho_buf.at[head], HO)

    load_wo.wait()
    await_bytes(ho_buf, recv_sem.at[HO])
    heads_out = jnp.concatenate([ho_buf[h] for h in range(QG)], axis=1)
    y = jnp.dot(heads_out, wo_v[...], preferred_element_type=F32)
    fin_buf[tp] = y.astype(BF16)
    for i, k in tp_steps:
        to = 2 * lax.rem(x + i, 4) + k
        if i == 0:

            @pl.when(to != tp)
            def _():
                send(fin_buf.at[tp], fin_buf.at[tp], FIN, FIN, tp=to)

        else:
            send(fin_buf.at[tp], fin_buf.at[tp], FIN, FIN, tp=to)
    await_bytes(fin_buf.at[pl.ds(0, ntp - 1)], recv_sem.at[FIN])
    att = jnp.sum(fin_buf[...].astype(F32), axis=0)
    for s in range(STEPS):
        out_ref[s, :, :width] = att[s * ROWS : (s + 1) * ROWS].astype(BF16)

    @pl.when(own_sum)
    def _():
        await_bytes(part_src.at[pl.ds(0, QG - 1)], send_sem.at[PART])
        await_bytes(sq_buf.at[pl.ds(0, QG - 1)], send_sem.at[SQ])

    @pl.when(jnp.logical_not(own_sum))
    def _():
        await_bytes(part_src.at[pl.ds(0, QG)], send_sem.at[PART])
        await_bytes(sq_buf.at[pl.ds(0, QG)], send_sem.at[SQ])

    @pl.when(own_kv)
    def _():
        await_bytes(part_src.at[pl.ds(0, 1)], send_sem.at[PART_KV])

    @pl.when(jnp.logical_not(own_kv))
    def _():
        await_bytes(part_src.at[pl.ds(0, 2)], send_sem.at[PART_KV])

    for does, phase in ((sums, PROJ), (sums_kv, PROJ_KV)):

        @pl.when(jnp.logical_and(does, parity == 1))
        def _():
            await_bytes(o_buf.at[pl.ds(0, nctx - 1)], send_sem.at[phase])

        @pl.when(jnp.logical_and(does, parity == 0))
        def _():
            await_bytes(o_buf, send_sem.at[phase])

    @pl.when(joins)
    def _():
        await_bytes(st_src.at[pl.ds(0, QG - 1)], send_sem.at[ST])
        await_bytes(o_src.at[pl.ds(0, QG - 1)], send_sem.at[OUT])
        await_bytes(o_buf.at[pl.ds(0, nctx - 1)], send_sem.at[HO])

    @pl.when(jnp.logical_not(joins))
    def _():
        await_bytes(st_src, send_sem.at[ST])
        await_bytes(o_src, send_sem.at[OUT])

    await_bytes(fin_buf.at[pl.ds(0, ntp - 1)], send_sem.at[FIN])


def local(nctx, ntp, inputs, norm_gain, w_query, w_key, w_value, w_out, key_cache, value_cache):
    depth = inputs.shape[2]
    width = w_out.shape[1]
    cached = key_cache.shape[1]
    hbm = pl.BlockSpec(memory_space=pltpu.HBM)
    vmem = pl.BlockSpec(memory_space=pltpu.VMEM)
    results = pl.pallas_call(
        functools.partial(kernel, nctx, ntp),
        out_shape=jax.ShapeDtypeStruct((STEPS, ROWS, width + 2 * HD), BF16),
        in_specs=[hbm] * 8,
        out_specs=vmem,
        scratch_shapes=[
            pltpu.VMEM((STEPS, ROWS, depth), BF16),
            pltpu.VMEM((1, depth), F32),
            pltpu.VMEM((depth, QG * HD), BF16),
            pltpu.VMEM((depth, 2 * HD), BF16),
            pltpu.VMEM((QG * HD, width), BF16),
            pltpu.VMEM((ROWS, cached, HD), BF16),
            pltpu.VMEM((ROWS, HD, cached), BF16),
            pltpu.VMEM((ROWS, cached, HD), BF16),
            pltpu.VMEM((1, HD), F32),
            pltpu.VMEM((nctx, 1, HD), F32),
            pltpu.VMEM((TILES, M, HD), F32),
            pltpu.VMEM((nctx, M, HD), F32),
            pltpu.VMEM((nctx, M, HD), F32),
            pltpu.VMEM((M, HD), BF16),
            pltpu.VMEM((M, HD), BF16),
            pltpu.VMEM((TILES, M, HD), BF16),
            pltpu.VMEM((QG * M, HD), F32),
            pltpu.VMEM((QG * M, HD), F32),
            pltpu.VMEM((ROWS, STEPS * QG, cached), BF16),
            pltpu.VMEM((QG, 1, HD), F32),
            pltpu.VMEM((nctx, 1, HD), F32),
            pltpu.VMEM((QG, M, HD), BF16),
            pltpu.VMEM((nctx, M, HD), BF16),
            pltpu.VMEM((M, HD), BF16),
            pltpu.VMEM((QG, M, HD), BF16),
            pltpu.VMEM((ntp, M, width), BF16),
            pltpu.SemaphoreType.DMA((8,)),
            pltpu.SemaphoreType.DMA((9,)),
            pltpu.SemaphoreType.DMA((9,)),
        ],
        compiler_params=pltpu.CompilerParams(
            collective_id=0, has_side_effects=True, vmem_limit_bytes=40 * 1024 * 1024
        ),
    )(
        *(
            pltpu.with_memory_space_constraint(operand, pltpu.HBM)
            for operand in (
                inputs,
                norm_gain.reshape(1, depth),
                w_query,
                w_key,
                w_value,
                w_out,
                key_cache,
                value_cache,
            )
        )
    )
    return (
        results[:, :, :width],
        results[:, :, width : width + HD],
        results[:, :, width + HD :],
    )


def solution(mesh):
    placed = (
        P(None, None, "ctx"),
        P("ctx"),
        P("ctx", "tp"),
        P("ctx", "tp"),
        P("ctx", "tp"),
        P("tp", "ctx"),
        P(None, "ctx", "tp"),
        P(None, "ctx", "tp"),
    )
    return jax.shard_map(
        functools.partial(local, mesh.shape["ctx"], mesh.shape["tp"]),
        mesh=mesh,
        in_specs=placed,
        out_specs=(P(None, None, "ctx"), P(None, None, "tp"), P(None, None, "tp")),
        check_vma=False,
    )
```

```python
import functools

import jax
import jax.numpy as jnp
from jax import lax
from jax.experimental import pallas as pl
from jax.experimental.pallas import tpu as pltpu
from jax.sharding import PartitionSpec as P

QG = 16
HD = 128
STEPS = 2
ROWS = 8
M = STEPS * ROWS
TILES = QG + 2
LOG2E = 1.4426950408889634
F32 = jnp.float32
BF16 = jnp.bfloat16


STEPS_AWAY = sorted(
    ((dy, dz) for dy in range(4) for dz in range(8) if (dy, dz) != (0, 0)),
    key=lambda step: -(min(step[0], 4 - step[0]) + min(step[1], 8 - step[1])),
)
def head_of(y, z):
    near = lax.rem(z + 2, 8)
    low = jnp.where(near < 6, y * 6 + near, QG)
    return jnp.where(y < 2, low, jnp.where(y == 3, jnp.where(z < 3, 12 + z, QG), 15 + z))


def kernel(
    nctx,
    ntp,
    x_hbm,
    gain_hbm,
    wq_hbm,
    wk_hbm,
    wv_hbm,
    wo_hbm,
    kc_hbm,
    vc_hbm,
    out_ref,
    x_v,
    gain_v,
    wq_v,
    wkv_v,
    wo_v,
    kc_v,
    kt_v,
    vc_v,
    sq_src,
    sq_buf,
    part_src,
    part_buf,
    kv_buf,
    proj_src,
    kv_src,
    proj_buf,
    q_rows,
    o_rows,
    p_v,
    st_src,
    st_buf,
    o_src,
    o_buf,
    ho_src,
    ho_buf,
    fin_buf,
    load_sem,
    send_sem,
    recv_sem,
):
    me = lax.axis_index("ctx")
    tp = lax.axis_index("tp")
    y, z, core = me // 8, lax.rem(me, 8), lax.rem(tp, 2)
    chip_tp = tp - core
    depth = x_v.shape[2]
    width = wo_v.shape[1]
    SQ, PART, PART_KV, PROJ, PROJ_KV, ST, OUT, HO, FIN = range(9)

    parity = lax.rem(y + z, 2)
    tile = y * 4 + z // 2
    sums = core == 1
    sums_kv = jnp.logical_and(sums, jnp.logical_and(y < 2, z < 2))
    own_sum = jnp.logical_and(sums, parity == 1)
    sibling_sum = jnp.logical_and(core == 0, parity == 0)
    group_tp = chip_tp + parity
    head = head_of(y, z)
    joins = head < QG

    def others():
        for dy, dz in STEPS_AWAY:
            ty, tz = lax.rem(y + dy, 4), lax.rem(z + dz, 8)
            yield ty * 8 + tz, ty, tz

    x = tp // 2
    tp_steps = [(i, k) for k in (1, 0) for i in (2, 1, 3, 0)]

    barrier = pltpu.get_barrier_semaphore()

    @pl.when(sums)
    def _():
        for to, _, _ in others():
            pl.semaphore_signal(barrier, inc=1, device_id={"ctx": to, "tp": group_tp})

        @pl.when(parity == 0)
        def _():
            pl.semaphore_signal(barrier, inc=1, device_id={"ctx": me, "tp": group_tp})

    for i in range(1, ntp):
        pl.semaphore_signal(barrier, inc=1, device_id={"tp": lax.rem(tp + i, ntp)})

    def load(i, src, dst):
        copy = pltpu.make_async_copy(src, dst, load_sem.at[i])
        copy.start()
        return copy

    load_x = load(0, x_hbm, x_v)
    load_gain = load(1, gain_hbm, gain_v)
    chunk = depth // 4
    load_q = [
        load(2 + i, wq_hbm.at[pl.ds(i * chunk, chunk)], wq_v.at[pl.ds(i * chunk, chunk)])
        for i in range(4)
    ]
    load_k = load(6, wk_hbm, wkv_v.at[:, pl.ds(0, HD)])
    load_v = load(7, wv_hbm, wkv_v.at[:, pl.ds(HD, HD)])

    def send(src, dst, phase, recv, **where):
        pltpu.make_async_remote_copy(
            src_ref=src,
            dst_ref=dst,
            send_sem=send_sem.at[phase],
            recv_sem=recv_sem.at[recv],
            device_id=where,
        ).start()

    def keep(src, dst, recv):
        pltpu.make_async_copy(src, dst, recv_sem.at[recv]).start()

    def await_bytes(ref, sem):
        pltpu.make_async_copy(ref, ref, sem).wait()

    load_x.wait()
    load_gain.wait()
    hidden = jnp.concatenate([x_v[0].astype(F32), x_v[1].astype(F32)], axis=0)
    normed = (hidden * gain_v[...]).astype(BF16)
    diagonal = lax.broadcasted_iota(jnp.int32, (M, HD), 0) == lax.broadcasted_iota(
        jnp.int32, (M, HD), 1
    )
    squares = jnp.sum(hidden * hidden, axis=1, keepdims=True)
    sq_src[...] = jnp.sum(jnp.where(diagonal, squares, 0.0), axis=0, keepdims=True)
    half = depth // 2
    for copy in load_q[:2]:
        copy.wait()
    part = jnp.dot(normed[:, :half], wq_v[:half, :], preferred_element_type=F32)
    for copy in load_q[2:]:
        copy.wait()
    load_k.wait()
    load_v.wait()
    load_kc = load(0, kc_hbm, kc_v)
    load_vc = load(1, vc_hbm, vc_v)
    load_wo = load(2, wo_hbm, wo_v)
    part += jnp.dot(normed[:, half:], wq_v[half:, :], preferred_element_type=F32)
    for h in range(QG):
        part_src[h] = part[:, h * HD : (h + 1) * HD]
    @pl.when(own_sum)
    def _():
        pl.semaphore_wait(barrier, QG - 1 + ntp - 1)

    @pl.when(jnp.logical_not(own_sum))
    def _():
        pl.semaphore_wait(barrier, QG + ntp - 1)

    for odd in range(2):

        @pl.when(lax.rem(core + parity, 2) == odd)
        def _():
            for dy, dz in STEPS_AWAY:
                if (dy + dz) % 2 == odd:
                    ty, tz = lax.rem(y + dy, 4), lax.rem(z + dz, 8)
                    to, h = ty * 8 + tz, ty * 4 + tz // 2
                    send(part_src.at[h], part_buf.at[me], PART, PART, ctx=to, tp=chip_tp + 1)
                    send(sq_src, sq_buf.at[me], SQ, SQ, ctx=to, tp=chip_tp + 1)

    @pl.when(sibling_sum)
    def _():
        send(part_src.at[tile], part_buf.at[me], PART, PART, tp=chip_tp + 1)
        send(sq_src, sq_buf.at[me], SQ, SQ, tp=chip_tp + 1)

    @pl.when(own_sum)
    def _():
        keep(part_src.at[tile], part_buf.at[me], PART)
        keep(sq_src, sq_buf.at[me], SQ)

    part = jnp.dot(normed, wkv_v[...], preferred_element_type=F32)
    for h in range(2):
        part_src[QG + h] = part[:, h * HD : (h + 1) * HD]

    load_kc.wait()

    @pl.loop(0, ROWS)
    def _(r):
        kt_v[r] = jnp.transpose(kc_v[r])

    def scale_of_rows():
        total = jnp.sum(sq_buf[...], axis=0)
        total = jnp.sum(jnp.where(diagonal, total, 0.0), axis=1, keepdims=True)
        return lax.rsqrt(total / (depth * nctx) + 1e-05)

    def broadcast(src, dst, phase):
        for to, _, _ in others():
            send(src, dst, phase, phase, ctx=to, tp=group_tp)

        @pl.when(parity == 0)
        def _():
            send(src, dst, phase, phase, tp=group_tp)

        @pl.when(parity == 1)
        def _():
            keep(src, dst, phase)

    @pl.when(sums)
    def _():
        await_bytes(sq_buf, recv_sem.at[SQ])
        scaling = scale_of_rows()
        await_bytes(part_buf, recv_sem.at[PART])
        proj_src[...] = (scaling * jnp.sum(part_buf[...], axis=0)).astype(BF16)
        broadcast(proj_src, proj_buf.at[tile], PROJ)

    own_kv = jnp.logical_and(sums_kv, own_sum)
    for i in range(2):
        to = 8 * i + lax.rem(i + core, 2)
        stays = jnp.logical_and(own_kv, y == i)

        @pl.when(stays)
        def _():
            keep(part_src.at[QG + i], kv_buf.at[me], PART_KV)

        @pl.when(jnp.logical_not(stays))
        def _():
            send(part_src.at[QG + i], kv_buf.at[me], PART_KV, PART_KV, ctx=to, tp=chip_tp + 1)

    await_bytes(proj_buf.at[pl.ds(0, QG)], recv_sem.at[PROJ])
    for h in range(QG):
        q_rows[pl.ds(h * M, M), :] = proj_buf[h].astype(F32)
    score_scale = LOG2E / float(HD) ** 0.5
    lane = lax.broadcasted_iota(jnp.int32, (QG, HD), 1)
    stats = jnp.zeros((QG, HD), F32)
    inverse = []
    for r in range(ROWS):
        q = jnp.concatenate(
            [q_rows[pl.ds(s * ROWS + r, QG, stride=M), :] for s in range(STEPS)], axis=0
        ).astype(BF16)
        score = jnp.dot(q, kt_v[r], preferred_element_type=F32)
        top = jnp.max(score, axis=1, keepdims=True)
        weight = jnp.exp2((score - top) * score_scale)
        total = jnp.sum(weight, axis=1, keepdims=True)
        p_v[r] = weight.astype(BF16)
        inverse.append(1.0 / total)
        lse = top * score_scale + jnp.log2(total)
        for s in range(STEPS):
            stats = jnp.where(lane == s * ROWS + r, lse[s * QG : (s + 1) * QG], stats)
    for h in range(QG):
        st_src[h] = stats[h : h + 1]

    load_vc.wait()
    for r in range(ROWS):
        out = jnp.dot(p_v[r], vc_v[r], preferred_element_type=F32) * inverse[r]
        for s in range(STEPS):
            o_rows[pl.ds(s * ROWS + r, QG, stride=M), :] = out[s * QG : (s + 1) * QG]
    for h in range(QG):
        o_src[h] = o_rows[pl.ds(h * M, M), :].astype(BF16)

    for to, ty, tz in others():
        h = head_of(ty, tz)

        @pl.when(h < QG)
        def _():
            send(st_src.at[h], st_buf.at[me], ST, ST, ctx=to)
            send(o_src.at[h], o_buf.at[me], OUT, OUT, ctx=to)

    @pl.when(joins)
    def _():
        keep(st_src.at[head], st_buf.at[me], ST)
        keep(o_src.at[head], o_buf.at[me], OUT)

    @pl.when(sums_kv)
    def _():
        await_bytes(kv_buf, recv_sem.at[PART_KV])
        kv_src[...] = (scale_of_rows() * jnp.sum(kv_buf[...], axis=0)).astype(BF16)
        broadcast(kv_src, proj_buf.at[QG + y], PROJ_KV)

    await_bytes(proj_buf.at[pl.ds(QG, 2)], recv_sem.at[PROJ_KV])
    new_k, new_v = proj_buf[QG].astype(F32), proj_buf[QG + 1].astype(F32)
    for s in range(STEPS):
        out_ref[s, :, width : width + HD] = new_k[s * ROWS : (s + 1) * ROWS].astype(BF16)
        out_ref[s, :, width + HD :] = new_v[s * ROWS : (s + 1) * ROWS].astype(BF16)

    @pl.when(joins)
    def _():
        second = lax.broadcasted_iota(jnp.int32, (M, 1), 0) >= ROWS
        q = proj_buf[head].astype(F32)
        k0 = jnp.concatenate([new_k[:ROWS]] * 2, axis=0)
        k1 = jnp.concatenate([new_k[ROWS:]] * 2, axis=0)
        v0 = jnp.concatenate([new_v[:ROWS]] * 2, axis=0)
        v1 = jnp.concatenate([new_v[ROWS:]] * 2, axis=0)
        f0 = jnp.sum(q * k0, axis=1, keepdims=True) * score_scale
        f1 = jnp.sum(q * k1, axis=1, keepdims=True) * score_scale
        await_bytes(st_buf, recv_sem.at[ST])
        lse = jnp.transpose(st_buf[...].reshape(nctx, HD))[:M]
        top = jnp.maximum(jnp.max(lse, axis=1, keepdims=True), f0)
        top = jnp.maximum(top, jnp.where(second, f1, f0))
        share = jnp.exp2(lse - top)
        w0 = jnp.exp2(f0 - top)
        w1 = jnp.where(second, jnp.exp2(jnp.where(second, f1, f0) - top), 0.0)
        over = 1.0 / (jnp.sum(share, axis=1, keepdims=True) + w0 + w1)
        joined = w0 * v0 + w1 * v1
        await_bytes(o_buf, recv_sem.at[OUT])
        for c in range(nctx):
            joined += share[:, c : c + 1] * o_buf[c].astype(F32)
        ho_src[...] = (joined * over).astype(BF16)
        @pl.when(me != 0)
        def _():
            send(ho_src, ho_buf.at[head], HO, HO, ctx=0)

        for to, _, _ in others():

            @pl.when(to != 0)
            def _():
                send(ho_src, ho_buf.at[head], HO, HO, ctx=to)

        keep(ho_src, ho_buf.at[head], HO)

    load_wo.wait()
    await_bytes(ho_buf, recv_sem.at[HO])
    heads_out = jnp.concatenate([ho_buf[h] for h in range(QG)], axis=1)
    y = jnp.dot(heads_out, wo_v[...], preferred_element_type=F32)
    fin_buf[tp] = y.astype(BF16)
    for i, k in tp_steps:
        to = 2 * lax.rem(x + i, 4) + k
        if i == 0:

            @pl.when(to != tp)
            def _():
                send(fin_buf.at[tp], fin_buf.at[tp], FIN, FIN, tp=to)

        else:
            send(fin_buf.at[tp], fin_buf.at[tp], FIN, FIN, tp=to)
    await_bytes(fin_buf.at[pl.ds(0, ntp - 1)], recv_sem.at[FIN])
    att = jnp.sum(fin_buf[...].astype(F32), axis=0)
    for s in range(STEPS):
        out_ref[s, :, :width] = att[s * ROWS : (s + 1) * ROWS].astype(BF16)

    @pl.when(own_sum)
    def _():
        await_bytes(part_src.at[pl.ds(0, QG - 1)], send_sem.at[PART])
        await_bytes(sq_buf.at[pl.ds(0, QG - 1)], send_sem.at[SQ])

    @pl.when(jnp.logical_not(own_sum))
    def _():
        await_bytes(part_src.at[pl.ds(0, QG)], send_sem.at[PART])
        await_bytes(sq_buf.at[pl.ds(0, QG)], send_sem.at[SQ])

    @pl.when(own_kv)
    def _():
        await_bytes(part_src.at[pl.ds(0, 1)], send_sem.at[PART_KV])

    @pl.when(jnp.logical_not(own_kv))
    def _():
        await_bytes(part_src.at[pl.ds(0, 2)], send_sem.at[PART_KV])

    for does, phase in ((sums, PROJ), (sums_kv, PROJ_KV)):

        @pl.when(jnp.logical_and(does, parity == 1))
        def _():
            await_bytes(o_buf.at[pl.ds(0, nctx - 1)], send_sem.at[phase])

        @pl.when(jnp.logical_and(does, parity == 0))
        def _():
            await_bytes(o_buf, send_sem.at[phase])

    @pl.when(joins)
    def _():
        await_bytes(st_src.at[pl.ds(0, QG - 1)], send_sem.at[ST])
        await_bytes(o_src.at[pl.ds(0, QG - 1)], send_sem.at[OUT])
        await_bytes(o_buf.at[pl.ds(0, nctx - 1)], send_sem.at[HO])

    @pl.when(jnp.logical_not(joins))
    def _():
        await_bytes(st_src, send_sem.at[ST])
        await_bytes(o_src, send_sem.at[OUT])

    await_bytes(fin_buf.at[pl.ds(0, ntp - 1)], send_sem.at[FIN])


def local(nctx, ntp, inputs, norm_gain, w_query, w_key, w_value, w_out, key_cache, value_cache):
    depth = inputs.shape[2]
    width = w_out.shape[1]
    cached = key_cache.shape[1]
    hbm = pl.BlockSpec(memory_space=pltpu.HBM)
    vmem = pl.BlockSpec(memory_space=pltpu.VMEM)
    results = pl.pallas_call(
        functools.partial(kernel, nctx, ntp),
        out_shape=jax.ShapeDtypeStruct((STEPS, ROWS, width + 2 * HD), BF16),
        in_specs=[hbm] * 8,
        out_specs=vmem,
        scratch_shapes=[
            pltpu.VMEM((STEPS, ROWS, depth), BF16),
            pltpu.VMEM((1, depth), F32),
            pltpu.VMEM((depth, QG * HD), BF16),
            pltpu.VMEM((depth, 2 * HD), BF16),
            pltpu.VMEM((QG * HD, width), BF16),
            pltpu.VMEM((ROWS, cached, HD), BF16),
            pltpu.VMEM((ROWS, HD, cached), BF16),
            pltpu.VMEM((ROWS, cached, HD), BF16),
            pltpu.VMEM((1, HD), F32),
            pltpu.VMEM((nctx, 1, HD), F32),
            pltpu.VMEM((TILES, M, HD), F32),
            pltpu.VMEM((nctx, M, HD), F32),
            pltpu.VMEM((nctx, M, HD), F32),
            pltpu.VMEM((M, HD), BF16),
            pltpu.VMEM((M, HD), BF16),
            pltpu.VMEM((TILES, M, HD), BF16),
            pltpu.VMEM((QG * M, HD), F32),
            pltpu.VMEM((QG * M, HD), F32),
            pltpu.VMEM((ROWS, STEPS * QG, cached), BF16),
            pltpu.VMEM((QG, 1, HD), F32),
            pltpu.VMEM((nctx, 1, HD), F32),
            pltpu.VMEM((QG, M, HD), BF16),
            pltpu.VMEM((nctx, M, HD), BF16),
            pltpu.VMEM((M, HD), BF16),
            pltpu.VMEM((QG, M, HD), BF16),
            pltpu.VMEM((ntp, M, width), BF16),
            pltpu.SemaphoreType.DMA((8,)),
            pltpu.SemaphoreType.DMA((9,)),
            pltpu.SemaphoreType.DMA((9,)),
        ],
        compiler_params=pltpu.CompilerParams(
            collective_id=0, has_side_effects=True, vmem_limit_bytes=40 * 1024 * 1024
        ),
    )(
        *(
            pltpu.with_memory_space_constraint(operand, pltpu.HBM)
            for operand in (
                inputs,
                norm_gain.reshape(1, depth),
                w_query,
                w_key,
                w_value,
                w_out,
                key_cache,
                value_cache,
            )
        )
    )
    return (
        results[:, :, :width],
        results[:, :, width : width + HD],
        results[:, :, width + HD :],
    )


def solution(mesh):
    placed = (
        P(None, None, "ctx"),
        P("ctx"),
        P("ctx", "tp"),
        P("ctx", "tp"),
        P("ctx", "tp"),
        P("tp", "ctx"),
        P(None, "ctx", "tp"),
        P(None, "ctx", "tp"),
    )
    return jax.shard_map(
        functools.partial(local, mesh.shape["ctx"], mesh.shape["tp"]),
        mesh=mesh,
        in_specs=placed,
        out_specs=(P(None, None, "ctx"), P(None, None, "tp"), P(None, None, "tp")),
        check_vma=False,
    )
```

```python
import functools

import jax
import jax.numpy as jnp
from jax import lax
from jax.experimental import pallas as pl
from jax.experimental.pallas import tpu as pltpu
from jax.sharding import PartitionSpec as P

QG = 16
HD = 128
STEPS = 2
ROWS = 8
M = STEPS * ROWS
TILES = QG + 2
LOG2E = 1.4426950408889634
F32 = jnp.float32
BF16 = jnp.bfloat16


STEPS_AWAY = sorted(
    ((dy, dz) for dy in range(4) for dz in range(8) if (dy, dz) != (0, 0)),
    key=lambda step: -(min(step[0], 4 - step[0]) + min(step[1], 8 - step[1])),
)
def head_of(y, z):
    near = lax.rem(z + 2, 8)
    low = jnp.where(near < 6, y * 6 + near, QG)
    return jnp.where(y < 2, low, jnp.where(y == 3, jnp.where(z < 3, 12 + z, QG), 15 + z))


def kernel(
    nctx,
    ntp,
    x_hbm,
    gain_hbm,
    wq_hbm,
    wk_hbm,
    wv_hbm,
    wo_hbm,
    kc_hbm,
    vc_hbm,
    out_ref,
    x_v,
    gain_v,
    wq_v,
    wkv_v,
    wo_v,
    kc_v,
    kt_v,
    vc_v,
    sq_src,
    sq_buf,
    part_src,
    part_buf,
    kv_buf,
    proj_src,
    kv_src,
    proj_buf,
    q_rows,
    o_rows,
    p_v,
    st_src,
    st_buf,
    o_src,
    o_buf,
    ho_src,
    ho_buf,
    fin_buf,
    load_sem,
    send_sem,
    recv_sem,
):
    me = lax.axis_index("ctx")
    tp = lax.axis_index("tp")
    y, z, core = me // 8, lax.rem(me, 8), lax.rem(tp, 2)
    chip_tp = tp - core
    depth = x_v.shape[2]
    width = wo_v.shape[1]
    SQ, PART, PART_KV, PROJ, PROJ_KV, ST, OUT, HO, FIN = range(9)

    parity = lax.rem(y + z, 2)
    tile = y * 4 + z // 2
    sums = core == 1
    sums_kv = jnp.logical_and(sums, jnp.logical_and(y < 2, z < 2))
    own_sum = jnp.logical_and(sums, parity == 1)
    sibling_sum = jnp.logical_and(core == 0, parity == 0)
    group_tp = chip_tp + parity
    head = head_of(y, z)
    joins = head < QG

    def others():
        for dy, dz in STEPS_AWAY:
            ty, tz = lax.rem(y + dy, 4), lax.rem(z + dz, 8)
            yield ty * 8 + tz, ty, tz

    x = tp // 2
    tp_steps = [(i, k) for k in (1, 0) for i in (2, 1, 3, 0)]

    barrier = pltpu.get_barrier_semaphore()

    @pl.when(sums)
    def _():
        for to, _, _ in others():
            pl.semaphore_signal(barrier, inc=1, device_id={"ctx": to, "tp": group_tp})

        @pl.when(parity == 0)
        def _():
            pl.semaphore_signal(barrier, inc=1, device_id={"ctx": me, "tp": group_tp})

    for i in range(1, ntp):
        pl.semaphore_signal(barrier, inc=1, device_id={"tp": lax.rem(tp + i, ntp)})

    def load(i, src, dst):
        copy = pltpu.make_async_copy(src, dst, load_sem.at[i])
        copy.start()
        return copy

    load_x = load(0, x_hbm, x_v)
    load_gain = load(1, gain_hbm, gain_v)
    chunk = depth // 4
    load_q = [
        load(2 + i, wq_hbm.at[pl.ds(i * chunk, chunk)], wq_v.at[pl.ds(i * chunk, chunk)])
        for i in range(4)
    ]
    load_k = load(6, wk_hbm, wkv_v.at[:, pl.ds(0, HD)])
    load_v = load(7, wv_hbm, wkv_v.at[:, pl.ds(HD, HD)])

    def send(src, dst, phase, recv, **where):
        pltpu.make_async_remote_copy(
            src_ref=src,
            dst_ref=dst,
            send_sem=send_sem.at[phase],
            recv_sem=recv_sem.at[recv],
            device_id=where,
        ).start()

    def keep(src, dst, recv):
        pltpu.make_async_copy(src, dst, recv_sem.at[recv]).start()

    def await_bytes(ref, sem):
        pltpu.make_async_copy(ref, ref, sem).wait()

    load_x.wait()
    load_gain.wait()
    hidden = jnp.concatenate([x_v[0].astype(F32), x_v[1].astype(F32)], axis=0)
    normed = (hidden * gain_v[...]).astype(BF16)
    diagonal = lax.broadcasted_iota(jnp.int32, (M, HD), 0) == lax.broadcasted_iota(
        jnp.int32, (M, HD), 1
    )
    squares = jnp.sum(hidden * hidden, axis=1, keepdims=True)
    sq_src[...] = jnp.sum(jnp.where(diagonal, squares, 0.0), axis=0, keepdims=True)
    half = depth // 2
    for copy in load_q[:2]:
        copy.wait()
    part = jnp.dot(normed[:, :half], wq_v[:half, :], preferred_element_type=F32)
    for copy in load_q[2:]:
        copy.wait()
    load_k.wait()
    load_v.wait()
    load_kc = load(0, kc_hbm, kc_v)
    load_vc = load(1, vc_hbm, vc_v)
    load_wo = load(2, wo_hbm, wo_v)
    part += jnp.dot(normed[:, half:], wq_v[half:, :], preferred_element_type=F32)
    for h in range(QG):
        part_src[h] = part[:, h * HD : (h + 1) * HD]
    @pl.when(own_sum)
    def _():
        pl.semaphore_wait(barrier, QG - 1 + ntp - 1)

    @pl.when(jnp.logical_not(own_sum))
    def _():
        pl.semaphore_wait(barrier, QG + ntp - 1)

    for odd in range(2):

        @pl.when(lax.rem(core + parity, 2) == odd)
        def _():
            for dy, dz in STEPS_AWAY:
                if (dy + dz) % 2 == odd:
                    ty, tz = lax.rem(y + dy, 4), lax.rem(z + dz, 8)
                    to, h = ty * 8 + tz, ty * 4 + tz // 2
                    send(part_src.at[h], part_buf.at[me], PART, PART, ctx=to, tp=chip_tp + 1)
            for dy, dz in STEPS_AWAY:
                if (dy + dz) % 2 == odd:
                    to = lax.rem(y + dy, 4) * 8 + lax.rem(z + dz, 8)
                    send(sq_src, sq_buf.at[me], SQ, SQ, ctx=to, tp=chip_tp + 1)

    @pl.when(sibling_sum)
    def _():
        send(part_src.at[tile], part_buf.at[me], PART, PART, tp=chip_tp + 1)
        send(sq_src, sq_buf.at[me], SQ, SQ, tp=chip_tp + 1)

    @pl.when(own_sum)
    def _():
        keep(part_src.at[tile], part_buf.at[me], PART)
        keep(sq_src, sq_buf.at[me], SQ)

    part = jnp.dot(normed, wkv_v[...], preferred_element_type=F32)
    for h in range(2):
        part_src[QG + h] = part[:, h * HD : (h + 1) * HD]

    load_kc.wait()

    @pl.loop(0, ROWS)
    def _(r):
        kt_v[r] = jnp.transpose(kc_v[r])

    def scale_of_rows():
        total = jnp.sum(sq_buf[...], axis=0)
        total = jnp.sum(jnp.where(diagonal, total, 0.0), axis=1, keepdims=True)
        return lax.rsqrt(total / (depth * nctx) + 1e-05)

    def broadcast(src, dst, phase):
        for to, _, _ in others():
            send(src, dst, phase, phase, ctx=to, tp=group_tp)

        @pl.when(parity == 0)
        def _():
            send(src, dst, phase, phase, tp=group_tp)

        @pl.when(parity == 1)
        def _():
            keep(src, dst, phase)

    @pl.when(sums)
    def _():
        await_bytes(sq_buf, recv_sem.at[SQ])
        scaling = scale_of_rows()
        await_bytes(part_buf, recv_sem.at[PART])
        proj_src[...] = (scaling * jnp.sum(part_buf[...], axis=0)).astype(BF16)
        broadcast(proj_src, proj_buf.at[tile], PROJ)

    own_kv = jnp.logical_and(sums_kv, own_sum)
    for i in range(2):
        to = 8 * i + lax.rem(i + core, 2)
        stays = jnp.logical_and(own_kv, y == i)

        @pl.when(stays)
        def _():
            keep(part_src.at[QG + i], kv_buf.at[me], PART_KV)

        @pl.when(jnp.logical_not(stays))
        def _():
            send(part_src.at[QG + i], kv_buf.at[me], PART_KV, PART_KV, ctx=to, tp=chip_tp + 1)

    await_bytes(proj_buf.at[pl.ds(0, QG)], recv_sem.at[PROJ])
    for h in range(QG):
        q_rows[pl.ds(h * M, M), :] = proj_buf[h].astype(F32)
    score_scale = LOG2E / float(HD) ** 0.5
    lane = lax.broadcasted_iota(jnp.int32, (QG, HD), 1)
    stats = jnp.zeros((QG, HD), F32)
    inverse = []
    for r in range(ROWS):
        q = jnp.concatenate(
            [q_rows[pl.ds(s * ROWS + r, QG, stride=M), :] for s in range(STEPS)], axis=0
        ).astype(BF16)
        score = jnp.dot(q, kt_v[r], preferred_element_type=F32)
        top = jnp.max(score, axis=1, keepdims=True)
        weight = jnp.exp2((score - top) * score_scale)
        total = jnp.sum(weight, axis=1, keepdims=True)
        p_v[r] = weight.astype(BF16)
        inverse.append(1.0 / total)
        lse = top * score_scale + jnp.log2(total)
        for s in range(STEPS):
            stats = jnp.where(lane == s * ROWS + r, lse[s * QG : (s + 1) * QG], stats)
    for h in range(QG):
        st_src[h] = stats[h : h + 1]

    load_vc.wait()
    for r in range(ROWS):
        out = jnp.dot(p_v[r], vc_v[r], preferred_element_type=F32) * inverse[r]
        for s in range(STEPS):
            o_rows[pl.ds(s * ROWS + r, QG, stride=M), :] = out[s * QG : (s + 1) * QG]
    for h in range(QG):
        o_src[h] = o_rows[pl.ds(h * M, M), :].astype(BF16)

    for to, ty, tz in others():
        h = head_of(ty, tz)

        @pl.when(h < QG)
        def _():
            send(st_src.at[h], st_buf.at[me], ST, ST, ctx=to)
            send(o_src.at[h], o_buf.at[me], OUT, OUT, ctx=to)

    @pl.when(joins)
    def _():
        keep(st_src.at[head], st_buf.at[me], ST)
        keep(o_src.at[head], o_buf.at[me], OUT)

    @pl.when(sums_kv)
    def _():
        await_bytes(kv_buf, recv_sem.at[PART_KV])
        kv_src[...] = (scale_of_rows() * jnp.sum(kv_buf[...], axis=0)).astype(BF16)
        broadcast(kv_src, proj_buf.at[QG + y], PROJ_KV)

    await_bytes(proj_buf.at[pl.ds(QG, 2)], recv_sem.at[PROJ_KV])
    new_k, new_v = proj_buf[QG].astype(F32), proj_buf[QG + 1].astype(F32)
    for s in range(STEPS):
        out_ref[s, :, width : width + HD] = new_k[s * ROWS : (s + 1) * ROWS].astype(BF16)
        out_ref[s, :, width + HD :] = new_v[s * ROWS : (s + 1) * ROWS].astype(BF16)

    @pl.when(joins)
    def _():
        second = lax.broadcasted_iota(jnp.int32, (M, 1), 0) >= ROWS
        q = proj_buf[head].astype(F32)
        k0 = jnp.concatenate([new_k[:ROWS]] * 2, axis=0)
        k1 = jnp.concatenate([new_k[ROWS:]] * 2, axis=0)
        v0 = jnp.concatenate([new_v[:ROWS]] * 2, axis=0)
        v1 = jnp.concatenate([new_v[ROWS:]] * 2, axis=0)
        f0 = jnp.sum(q * k0, axis=1, keepdims=True) * score_scale
        f1 = jnp.sum(q * k1, axis=1, keepdims=True) * score_scale
        await_bytes(st_buf, recv_sem.at[ST])
        lse = jnp.transpose(st_buf[...].reshape(nctx, HD))[:M]
        top = jnp.maximum(jnp.max(lse, axis=1, keepdims=True), f0)
        top = jnp.maximum(top, jnp.where(second, f1, f0))
        share = jnp.exp2(lse - top)
        w0 = jnp.exp2(f0 - top)
        w1 = jnp.where(second, jnp.exp2(jnp.where(second, f1, f0) - top), 0.0)
        over = 1.0 / (jnp.sum(share, axis=1, keepdims=True) + w0 + w1)
        joined = w0 * v0 + w1 * v1
        await_bytes(o_buf, recv_sem.at[OUT])
        for c in range(nctx):
            joined += share[:, c : c + 1] * o_buf[c].astype(F32)
        ho_src[...] = (joined * over).astype(BF16)
        @pl.when(me != 0)
        def _():
            send(ho_src, ho_buf.at[head], HO, HO, ctx=0)

        for to, _, _ in others():

            @pl.when(to != 0)
            def _():
                send(ho_src, ho_buf.at[head], HO, HO, ctx=to)

        keep(ho_src, ho_buf.at[head], HO)

    load_wo.wait()
    await_bytes(ho_buf, recv_sem.at[HO])
    heads_out = jnp.concatenate([ho_buf[h] for h in range(QG)], axis=1)
    y = jnp.dot(heads_out, wo_v[...], preferred_element_type=F32)
    fin_buf[tp] = y.astype(BF16)
    for i, k in tp_steps:
        to = 2 * lax.rem(x + i, 4) + k
        if i == 0:

            @pl.when(to != tp)
            def _():
                send(fin_buf.at[tp], fin_buf.at[tp], FIN, FIN, tp=to)

        else:
            send(fin_buf.at[tp], fin_buf.at[tp], FIN, FIN, tp=to)
    await_bytes(fin_buf.at[pl.ds(0, ntp - 1)], recv_sem.at[FIN])
    att = jnp.sum(fin_buf[...].astype(F32), axis=0)
    for s in range(STEPS):
        out_ref[s, :, :width] = att[s * ROWS : (s + 1) * ROWS].astype(BF16)

    @pl.when(own_sum)
    def _():
        await_bytes(part_src.at[pl.ds(0, QG - 1)], send_sem.at[PART])
        await_bytes(sq_buf.at[pl.ds(0, QG - 1)], send_sem.at[SQ])

    @pl.when(jnp.logical_not(own_sum))
    def _():
        await_bytes(part_src.at[pl.ds(0, QG)], send_sem.at[PART])
        await_bytes(sq_buf.at[pl.ds(0, QG)], send_sem.at[SQ])

    @pl.when(own_kv)
    def _():
        await_bytes(part_src.at[pl.ds(0, 1)], send_sem.at[PART_KV])

    @pl.when(jnp.logical_not(own_kv))
    def _():
        await_bytes(part_src.at[pl.ds(0, 2)], send_sem.at[PART_KV])

    for does, phase in ((sums, PROJ), (sums_kv, PROJ_KV)):

        @pl.when(jnp.logical_and(does, parity == 1))
        def _():
            await_bytes(o_buf.at[pl.ds(0, nctx - 1)], send_sem.at[phase])

        @pl.when(jnp.logical_and(does, parity == 0))
        def _():
            await_bytes(o_buf, send_sem.at[phase])

    @pl.when(joins)
    def _():
        await_bytes(st_src.at[pl.ds(0, QG - 1)], send_sem.at[ST])
        await_bytes(o_src.at[pl.ds(0, QG - 1)], send_sem.at[OUT])
        await_bytes(o_buf.at[pl.ds(0, nctx - 1)], send_sem.at[HO])

    @pl.when(jnp.logical_not(joins))
    def _():
        await_bytes(st_src, send_sem.at[ST])
        await_bytes(o_src, send_sem.at[OUT])

    await_bytes(fin_buf.at[pl.ds(0, ntp - 1)], send_sem.at[FIN])


def local(nctx, ntp, inputs, norm_gain, w_query, w_key, w_value, w_out, key_cache, value_cache):
    depth = inputs.shape[2]
    width = w_out.shape[1]
    cached = key_cache.shape[1]
    hbm = pl.BlockSpec(memory_space=pltpu.HBM)
    vmem = pl.BlockSpec(memory_space=pltpu.VMEM)
    results = pl.pallas_call(
        functools.partial(kernel, nctx, ntp),
        out_shape=jax.ShapeDtypeStruct((STEPS, ROWS, width + 2 * HD), BF16),
        in_specs=[hbm] * 8,
        out_specs=vmem,
        scratch_shapes=[
            pltpu.VMEM((STEPS, ROWS, depth), BF16),
            pltpu.VMEM((1, depth), F32),
            pltpu.VMEM((depth, QG * HD), BF16),
            pltpu.VMEM((depth, 2 * HD), BF16),
            pltpu.VMEM((QG * HD, width), BF16),
            pltpu.VMEM((ROWS, cached, HD), BF16),
            pltpu.VMEM((ROWS, HD, cached), BF16),
            pltpu.VMEM((ROWS, cached, HD), BF16),
            pltpu.VMEM((1, HD), F32),
            pltpu.VMEM((nctx, 1, HD), F32),
            pltpu.VMEM((TILES, M, HD), F32),
            pltpu.VMEM((nctx, M, HD), F32),
            pltpu.VMEM((nctx, M, HD), F32),
            pltpu.VMEM((M, HD), BF16),
            pltpu.VMEM((M, HD), BF16),
            pltpu.VMEM((TILES, M, HD), BF16),
            pltpu.VMEM((QG * M, HD), F32),
            pltpu.VMEM((QG * M, HD), F32),
            pltpu.VMEM((ROWS, STEPS * QG, cached), BF16),
            pltpu.VMEM((QG, 1, HD), F32),
            pltpu.VMEM((nctx, 1, HD), F32),
            pltpu.VMEM((QG, M, HD), BF16),
            pltpu.VMEM((nctx, M, HD), BF16),
            pltpu.VMEM((M, HD), BF16),
            pltpu.VMEM((QG, M, HD), BF16),
            pltpu.VMEM((ntp, M, width), BF16),
            pltpu.SemaphoreType.DMA((8,)),
            pltpu.SemaphoreType.DMA((9,)),
            pltpu.SemaphoreType.DMA((9,)),
        ],
        compiler_params=pltpu.CompilerParams(
            collective_id=0, has_side_effects=True, vmem_limit_bytes=40 * 1024 * 1024
        ),
    )(
        *(
            pltpu.with_memory_space_constraint(operand, pltpu.HBM)
            for operand in (
                inputs,
                norm_gain.reshape(1, depth),
                w_query,
                w_key,
                w_value,
                w_out,
                key_cache,
                value_cache,
            )
        )
    )
    return (
        results[:, :, :width],
        results[:, :, width : width + HD],
        results[:, :, width + HD :],
    )


def solution(mesh):
    placed = (
        P(None, None, "ctx"),
        P("ctx"),
        P("ctx", "tp"),
        P("ctx", "tp"),
        P("ctx", "tp"),
        P("tp", "ctx"),
        P(None, "ctx", "tp"),
        P(None, "ctx", "tp"),
    )
    return jax.shard_map(
        functools.partial(local, mesh.shape["ctx"], mesh.shape["tp"]),
        mesh=mesh,
        in_specs=placed,
        out_specs=(P(None, None, "ctx"), P(None, None, "tp"), P(None, None, "tp")),
        check_vma=False,
    )
```
